512 devices in a mesh: lat: 32 (over y_hi, z, core), lon: 16 (over y_lo, x).
Axes of the slice: x: 4, y: 8 (y_hi: 2, y_lo: 4; y = y_hi * 4 + y_lo), z: 8, core: 2. Of those that a mesh axis runs over, the one named last changes fastest.
Arguments:
- tokens: bfloat16 [128, 1024, 768], P('lat', 'lon'), may hold values from -6 to 6
- source_id: int32 [128, 1024], P('lat', 'lon'), may hold values from 0 to 4
- valid: int32 [128, 1024], P('lat', 'lon'), may hold values 0 or 1
- source_table: float32 [5, 768], replicated, may hold values from -3 to 3
- gain_lon: float32 [768], replicated, may hold values from 0.25 to 1.75
- gain_lat: float32 [768], replicated, may hold values from 0.25 to 1.75
- wqkv_lon: bfloat16 [768, 2304], P('lat', 'lon'), may hold values from -0.21650635 to 0.21650635
- wout_lon: bfloat16 [768, 768], P('lat', 'lon'), may hold values from -0.21875 to 0.21875
- wqkv_lat: bfloat16 [768, 2304], P('lat', 'lon'), may hold values from -0.21650635 to 0.21650635
- wout_lat: bfloat16 [768, 768], P('lat', 'lon'), may hold values from -0.21875 to 0.21875
Outputs:
- mixed: bfloat16 [128, 1024, 768], P('lat', 'lon')
The draws below stay inside these ranges and needn't reach their ends.
All inputs are finite; a program needn't handle non-finite values. No bound on the sum of `valid` on one device may be relied on, other than what follows from the above.
Results may differ from the reference program's by a relative error of at most 0.0095.
Values may be sent and summed in bfloat16 or wider, within the bound.
A program may use at most 128 MiB of HBM per device.

```python
import jax
import jax.numpy as jnp
from jax import lax

D = 768
HEADS = 16
HD = 48
NSRC = 5
LAT = 128
LON = 1024


def drawn_weights(base_key):
    return jax.random.truncated_normal(base_key, -5.9, 5.9, (D, 3 * D), jnp.float32) * D ** (-0.5)


def draw_wqkv_lon(key, part):
    key = jax.random.fold_in(key, 11)
    base_key = jax.random.fold_in(key, 0)
    weights = drawn_weights(base_key)
    return weights.astype(jnp.bfloat16)


def draw_wqkv_lat(key, part):
    key = jax.random.fold_in(key, 23)
    base_key = jax.random.fold_in(key, 0)
    weights = drawn_weights(base_key)
    return weights.astype(jnp.bfloat16)


def place_ends(entries, stream_key, least, top_value):
    index_at = [jax.random.randint(jax.random.fold_in(stream_key, axis), (), 0, length) for axis, length in enumerate(entries.shape)]
    main_axis = entries.shape.index(max(entries.shape))
    next_to = index_at[:main_axis] + [(index_at[main_axis] + 1) % entries.shape[main_axis]] + index_at[main_axis + 1:]
    return entries.at[tuple(index_at)].set(least).at[tuple(next_to)].set(top_value)


def shard_levels(rng, shape, pieces, smallest, top_value):
    def one(position, blocks):
        steps = jax.random.uniform(jax.random.fold_in(jax.random.fold_in(rng, 6), position), (blocks,), jnp.float32, smallest / len(pieces), top_value / len(pieces))
        return jnp.repeat(jnp.exp(steps), shape[position] // blocks).reshape((-1,) + (1,) * (len(shape) - position - 1))

    level = one(*pieces[0])
    for cut in pieces[1:]:
        level = level * one(*cut)
    return level


def normal_values(stream_key, dims, spread, bound, cuts=(), kind=jnp.bfloat16):
    entries = jax.random.normal(stream_key, dims, jnp.float32) * spread
    if len(cuts) > 0:
        entries = shard_levels(stream_key, dims, cuts, -0.22, 0.18) * entries
    return jnp.clip(entries, min=-bound, max=bound).astype(kind)


def setup_inputs(seed: int = 0) -> dict:
    key_of = jax.random.split(jax.random.key(seed), 11)
    return {
        "tokens": normal_values(key_of[0], (LAT, LON, D), 1.0, 6.0, ((0, 32), (1, 16))),
        "source_id": place_ends(jax.random.randint(key_of[1], (LAT, LON), 0, NSRC), jax.random.fold_in(key_of[1], 1), 0, NSRC - 1).astype(jnp.int32),
        "valid": place_ends((jax.random.randint(key_of[2], (LAT, LON), 0, 4) < 3).astype(jnp.int32), jax.random.fold_in(key_of[2], 1), 0, 1),
        "source_table": normal_values(key_of[3], (NSRC, D), 0.5, 3.0, (), jnp.float32),
        "gain_lon": jnp.clip(1.0 + 0.15 * jax.random.normal(key_of[4], (D,), jnp.float32), 0.25, 1.75),
        "gain_lat": jnp.clip(1.0 + 0.15 * jax.random.normal(key_of[5], (D,), jnp.float32), 0.25, 1.75),
        "wqkv_lon": draw_wqkv_lon(jax.random.fold_in(key_of[10], 71), 0),
        "wout_lon": normal_values(key_of[7], (D, D), D ** -0.5, 0.21875, ((0, 32), (1, 16))),
        "wqkv_lat": draw_wqkv_lat(jax.random.fold_in(key_of[10], 71), 0),
        "wout_lat": normal_values(key_of[9], (D, D), D ** -0.5, 0.21875, ((0, 32), (1, 16))),
    }


def normalize(x, gain):
    scale = lax.rsqrt(lax.optimization_barrier(jnp.mean(x * x, axis=-1, keepdims=True)) + 1e-06)
    return (x * scale * gain).astype(jnp.bfloat16)

def attend_line(x, keep, gain, wqkv, wout):
    normed = normalize(x, gain)
    qkv = jnp.dot(normed, wqkv, preferred_element_type=jnp.float32).astype(jnp.bfloat16)
    qkv = qkv.reshape(x.shape[0], 3, HEADS, HD)
    query = qkv[:, 0].astype(jnp.float32)
    keys = qkv[:, 1].astype(jnp.float32)
    values = qkv[:, 2].astype(jnp.float32)
    scores = jnp.einsum('qhd,khd->hqk', query, keys) / jnp.sqrt(jnp.float32(HD))
    scores = jnp.where(keep[None, None, :] > 0, scores, jnp.float32(-1e+30))
    top = lax.optimization_barrier(jnp.max(scores, axis=-1, keepdims=True))
    expo = jnp.exp(scores - top)
    probs = (expo / lax.optimization_barrier(jnp.sum(expo, axis=-1, keepdims=True))).astype(jnp.bfloat16)
    heads_out = jnp.einsum('hqk,khd->qhd', probs.astype(jnp.float32), values).astype(jnp.bfloat16)
    heads_out = heads_out.reshape(x.shape[0], D)
    return x + jnp.dot(heads_out, wout, preferred_element_type=jnp.float32)

def reference(tokens, source_id, valid, source_table, gain_lon, gain_lat, wqkv_lon, wout_lon, wqkv_lat, wout_lat):
    start = tokens.astype(jnp.float32) + source_table[source_id]

    def along_row(item):
        return attend_line(item[0], item[1], gain_lon, wqkv_lon, wout_lon)
    middle = lax.map(along_row, (start, valid))

    def along_column(item):
        return attend_line(item[0], item[1], gain_lat, wqkv_lat, wout_lat).astype(jnp.bfloat16)
    mixed = lax.map(along_column, (jnp.swapaxes(middle, 0, 1), jnp.swapaxes(valid, 0, 1)))
    return jnp.swapaxes(mixed, 0, 1)
```

```python
import functools

import jax
import jax.numpy as jnp
from jax import lax
from jax.experimental import pallas as pl
from jax.experimental.pallas import tpu as pltpu
from jax.sharding import PartitionSpec as P

HEADS = 16
HD = 48
D = 768
NLAT = 32
NLON = 16
MESH = pl.DeviceIdType.MESH
BF = jnp.bfloat16
F32 = jnp.float32
ANY = pl.BlockSpec(memory_space=pl.ANY)
VMEM = pl.BlockSpec(memory_space=pltpu.VMEM)
DMA = pltpu.SemaphoreType.DMA
SCALE2 = float(1.4426950408889634 / (48.0**0.5))
LIMIT = 56 * 1024 * 1024


def normalize(x, gain):
    scale = lax.rsqrt(jnp.mean(x * x, axis=-1, keepdims=True) + 1e-06)
    return (x * scale * gain).astype(BF)


def where_am_i():
    return lax.axis_index("lat"), lax.axis_index("lon")


def remote(src, dst, send, recv, lat, lon):
    return pltpu.make_async_remote_copy(
        src_ref=src,
        dst_ref=dst,
        send_sem=send,
        recv_sem=recv,
        device_id=(lat, lon),
        device_id_type=MESH,
    )


def shifted(lat, lon, t, sign):
    core = lax.rem(lat, 2)
    dyi = t // 4
    off = dyi + 4 * (dyi // 3) + 4 * core * ((dyi // 2) * (3 - dyi))
    y = (lat // 16) * 4 + lon // 4
    y2 = lax.rem(y + off, 8) if sign > 0 else lax.rem(y + 8 - off, 8)
    dx = lax.rem(t, 4)
    x = lax.rem(lon, 4)
    x2 = lax.rem(x + dx, 4) if sign > 0 else lax.rem(x + 4 - dx, 4)
    return lax.rem(lat, 16) + 16 * (y2 // 4), lax.rem(y2, 4) * 4 + x2


def signal(sem, lat, lon):
    pl.semaphore_signal(sem, inc=1, device_id=(lat, lon), device_id_type=MESH)


def loop(lo, hi, body):
    def step(i, carry):
        body(i)
        return carry

    lax.fori_loop(lo, hi, step, 0)


def gather_lat_kernel(w_ref, v_ref, land, vlon, vlat, ws, wr, vls, vlr, vts, vtr):
    lat, lon = where_am_i()
    bar = pltpu.get_barrier_semaphore()
    loop(1, NLAT, lambda s: signal(bar, lax.rem(lat + s, NLAT), lon))
    loop(1, NLON, lambda s: signal(bar, lat, lax.rem(lon + s, NLON)))
    pl.semaphore_wait(bar, NLAT - 1 + NLON - 1)

    def wcopy(s):
        return remote(w_ref, land.at[lat], ws.at[s], wr.at[s], lax.rem(lat + s, NLAT), lon)

    def vtcopy(s):
        return remote(v_ref, vlat.at[lat], vts.at[s], vtr.at[s], lax.rem(lat + s, NLAT), lon)

    def vlcopy(s):
        return remote(v_ref, vlon.at[lon], vls.at[s], vlr.at[s], lat, lax.rem(lon + s, NLON))

    own = (
        pltpu.make_async_copy(w_ref, land.at[lat], wr.at[0]),
        pltpu.make_async_copy(v_ref, vlat.at[lat], vtr.at[0]),
        pltpu.make_async_copy(v_ref, vlon.at[lon], vlr.at[0]),
    )
    loop(1, NLAT, lambda s: wcopy(s).start())
    loop(1, NLON, lambda s: vlcopy(s).start())
    loop(1, NLAT, lambda s: vtcopy(s).start())
    for c in own:
        c.start()
    for c in own:
        c.wait()
    loop(1, NLAT, lambda s: wcopy(s).wait())
    loop(1, NLON, lambda s: vlcopy(s).wait())
    loop(1, NLAT, lambda s: vtcopy(s).wait())


def gather_lat(w, v):
    return pl.pallas_call(
        gather_lat_kernel,
        out_shape=(
            jax.ShapeDtypeStruct((NLAT, 24, 384), BF),
            jax.ShapeDtypeStruct((NLON, 8, 128), jnp.int32),
            jax.ShapeDtypeStruct((NLAT, 8, 128), jnp.int32),
        ),
        in_specs=[ANY, ANY],
        out_specs=(ANY, ANY, ANY),
        scratch_shapes=[DMA((NLAT,)), DMA((NLAT,)), DMA((NLON,)), DMA((NLON,)), DMA((NLAT,)), DMA((NLAT,))],
        compiler_params=pltpu.CompilerParams(collective_id=0, has_side_effects=True),
    )(w, v)


def head_unit(lon, i):
    u = lon * 3 + i
    return u // 16, lax.rem(u, 16)


def lon_in_kernel(x_ref, units, row, u1, ys, xs, rs, us, ur, own_sem):
    lat, lon = where_am_i()
    a, b = lon // 4, lax.rem(lon, 4)
    bar = pltpu.get_barrier_semaphore()

    def greet(t):
        p, q = shifted(lat, lon, t, 1)
        signal(bar, p, q)
        p, q = shifted(lat, lon, t, -1)
        signal(bar, p, q)

    loop(1, 16, greet)
    loop(1, 4, lambda s: signal(bar, lat, lax.rem(a + s, 4) * 4 + b))
    loop(1, 4, lambda s: signal(bar, lat, a * 4 + lax.rem(b + s, 4)))
    pl.semaphore_wait(bar, 36)

    def ycopy(s):
        to = lax.rem(a + s, 4)
        return remote(x_ref.at[to], row.at[b, a], ys.at[s], rs.at[b, a], lat, to * 4 + b)

    loop(1, 4, lambda s: ycopy(s).start())
    own = pltpu.make_async_copy(x_ref.at[a], row.at[b, a], own_sem)
    own.start()

    def each_unit(act):
        for i in range(3):
            part, h = head_unit(lon, i)
            slot = part * 4 + lax.rem(h, 4)
            g = h // 4

            def dest(dyi):
                t = dyi * 4 + lax.rem(g - b + 4, 4)
                p, q = shifted(lat, lon, t, 1)
                mine = t == 0
                far = remote(units.at[i], u1.at[slot], us.at[i, dyi], ur.at[slot], p, q)
                near = pltpu.make_async_copy(units.at[i], u1.at[slot], ur.at[slot])
                act(mine, far, near)

            loop(0, 4, dest)

    def begin(mine, far, near):
        @pl.when(mine)
        def _():
            near.start()

        @pl.when(jnp.logical_not(mine))
        def _():
            far.start()

    def finish(mine, far, near):
        @pl.when(jnp.logical_not(mine))
        def _():
            far.wait_send()

    each_unit(begin)
    own.wait()

    def xcopy(s, aa):
        to = lax.rem(b + s, 4)
        return remote(row.at[b, aa], row.at[b, aa], xs.at[s, aa], rs.at[b, aa], lat, a * 4 + to)

    def landed(bb, aa):
        return pltpu.make_async_copy(row.at[bb, aa], row.at[bb, aa], rs.at[bb, aa])

    loop(1, 4, lambda s: xcopy(s, a).start())

    def forward(s):
        src = lax.rem(a + 4 - s, 4)
        landed(b, src).wait()
        loop(1, 4, lambda k: xcopy(k, src).start())

    loop(1, 4, forward)

    def collect(s):
        src = lax.rem(b + s, 4)
        loop(0, 4, lambda aa: landed(src, aa).wait())

    loop(1, 4, collect)
    loop(0, 12, lambda k: pltpu.make_async_copy(u1.at[k], u1.at[k], ur.at[k]).wait())
    loop(1, 4, lambda s: ycopy(s).wait_send())
    loop(1, 4, lambda s: loop(0, 4, lambda aa: xcopy(s, aa).wait_send()))
    each_unit(finish)


def lon_in(x, units):
    return pl.pallas_call(
        lon_in_kernel,
        out_shape=(
            jax.ShapeDtypeStruct((4, 4, 64, D), BF),
            jax.ShapeDtypeStruct((12, HD, D), BF),
        ),
        in_specs=[ANY, ANY],
        out_specs=(ANY, ANY),
        scratch_shapes=[DMA((4,)), DMA((4, 4)), DMA((4, 4)), DMA((3, 4)), DMA((12,)), DMA],
        compiler_params=pltpu.CompilerParams(collective_id=1, has_side_effects=True),
    )(x, units)


def soft(k_aug, q_aug, v_aug):
    s = lax.dot_general(k_aug, q_aug, (((0,), (0,)), ((), ())), preferred_element_type=F32)
    m = jnp.max(s, axis=0, keepdims=True)
    p = jnp.exp2((s - m) * SCALE2).astype(BF)
    o = jnp.dot(v_aug, p, preferred_element_type=F32)
    return o[:HD] / o[HD : HD + 1]


def lon_attend_kernel(
    x_ref, w_ref, ka_ref, qa_ref, units, land, wo1, u2, wo2,
    q_s, kv_s, t_s, o_s, os, orr, s1, r1, s2, r2, s3, r3,
):
    lat, lon = where_am_i()
    a, b = lon // 4, lax.rem(lon, 4)
    core = lax.rem(lat, 2)
    bar = pltpu.get_barrier_semaphore()

    def greet(t):
        p, q = shifted(lat, lon, t, 1)
        signal(bar, p, q)
        p, q = shifted(lat, lon, t, -1)
        signal(bar, p, q)
        signal(bar, lat, lax.rem(lon + t, NLON))

    loop(1, 16, greet)
    pl.semaphore_wait(bar, 45)

    def wo1copy(t):
        p, q = shifted(lat, lon, t, 1)
        return remote(units.at[3], wo1.at[lon], s1.at[t], r1.at[lon], p, q)

    def wo2copy(t):
        p, q = shifted(lat, lon, t, 1)
        return remote(units.at[7], wo2.at[lon], s2.at[t], r2.at[lon], p, q)

    own1 = pltpu.make_async_copy(units.at[3], wo1.at[lon], r1.at[lon])
    own2 = pltpu.make_async_copy(units.at[7], wo2.at[lon], r2.at[lon])
    own1.start()
    own2.start()

    def u2do(act):
        for i in range(3):
            part, h = head_unit(lon, i)
            slot = part * 8 + lax.rem(h, 8)

            @pl.when(h // 8 == core)
            def _():
                def one(t):
                    p, q = shifted(lat, lon, t, 1)
                    c = remote(units.at[4 + i], u2.at[slot], s3.at[i, t], r3.at[slot], p, q)
                    if act == "start":
                        c.start()
                    else:
                        c.wait_send()

                loop(1, 16, one)
                if act == "start":
                    pltpu.make_async_copy(units.at[4 + i], u2.at[slot], r3.at[slot]).start()

    loop(1, 16, lambda t: wo1copy(t).start())
    u2do("start")
    loop(1, 16, lambda t: wo2copy(t).start())

    qkv = lax.dot_general(
        w_ref[...], x_ref[...], (((1,), (1,)), ((), ())), preferred_element_type=F32
    ).astype(BF)
    for h in range(4):
        for qb in range(4):
            q_s[qb, h] = qkv[h * HD : (h + 1) * HD, qb * 256 : (qb + 1) * 256]
        kv_s[h] = qkv[192 + h * HD : 192 + (h + 1) * HD]
        kv_s[4 + h] = qkv[384 + h * HD : 384 + (h + 1) * HD]
    o_s[...] = jnp.zeros_like(o_s)

    def ocopy(bb, aa):
        far = remote(o_s.at[bb, aa], land.at[lon], os.at[bb, aa], orr.at[lon], lat, aa * 4 + bb)
        near = pltpu.make_async_copy(o_s.at[bb, aa], land.at[lon], orr.at[lon])
        return aa * 4 + bb == lon, far, near

    def block(qb):
        def head(h):
            k_aug = jnp.concatenate([kv_s[h], ka_ref[...]], axis=0)
            q_aug = jnp.concatenate([q_s[qb, h], qa_ref[...]], axis=0)
            v_aug = jnp.concatenate([kv_s[4 + h], jnp.ones((16, 1024), BF)], axis=0)
            t_s[h] = soft(k_aug, q_aug, v_aug)

        loop(0, 4, head)
        o = jnp.transpose(t_s[...].reshape(192, 256)).astype(BF)
        for aa in range(4):
            o_s[qb, aa, :, :192] = o[aa * 64 : (aa + 1) * 64]

        def send(aa):
            mine, far, near = ocopy(qb, aa)

            @pl.when(mine)
            def _():
                near.start()

            @pl.when(jnp.logical_not(mine))
            def _():
                far.start()

        loop(0, 4, send)

    loop(0, 4, block)

    def done(qb):
        def one(aa):
            mine, far, near = ocopy(qb, aa)

            @pl.when(jnp.logical_not(mine))
            def _():
                far.wait_send()

        loop(0, 4, one)

    loop(0, 4, done)
    loop(0, 16, lambda k: pltpu.make_async_copy(land.at[k], land.at[k], orr.at[k]).wait())
    loop(0, 16, lambda k: pltpu.make_async_copy(wo1.at[k], wo1.at[k], r1.at[k]).wait())
    loop(0, 16, lambda k: pltpu.make_async_copy(wo2.at[k], wo2.at[k], r2.at[k]).wait())
    loop(0, 24, lambda k: pltpu.make_async_copy(u2.at[k], u2.at[k], r3.at[k]).wait())
    loop(1, 16, lambda t: wo1copy(t).wait_send())
    loop(1, 16, lambda t: wo2copy(t).wait_send())
    u2do("finish")


def lon_attend(x, w, ka, qa, units):
    return pl.pallas_call(
        lon_attend_kernel,
        out_shape=(
            jax.ShapeDtypeStruct((NLON, 64, 256), BF),
            jax.ShapeDtypeStruct((16, HD, D), BF),
            jax.ShapeDtypeStruct((24, HD, D), BF),
            jax.ShapeDtypeStruct((16, HD, D), BF),
        ),
        in_specs=[VMEM, VMEM, VMEM, VMEM, ANY],
        out_specs=(ANY, ANY, ANY, ANY),
        scratch_shapes=[
            pltpu.VMEM((4, 4, HD, 256), BF),
            pltpu.VMEM((8, HD, 1024), BF),
            pltpu.VMEM((4, HD, 256), F32),
            pltpu.VMEM((4, 4, 64, 256), BF),
            DMA((4, 4)), DMA((16,)), DMA((16,)), DMA((16,)), DMA((16,)), DMA((16,)), DMA((3, 16)), DMA((24,)),
        ],
        compiler_params=pltpu.CompilerParams(
            collective_id=2, has_side_effects=True, vmem_limit_bytes=LIMIT
        ),
    )(x, w, ka, qa, units)


def lat_attend_kernel(x_ref, w_ref, ka_ref, qa_ref, back, col, qkv_s, t_s, o_s, xs, xr, bs, br):
    lat, lon = where_am_i()
    bar = pltpu.get_barrier_semaphore()
    loop(1, NLAT, lambda s: signal(bar, lax.rem(lat + s, NLAT), lon))
    pl.semaphore_wait(bar, NLAT - 1)

    def xcopy(s):
        to = lax.rem(lat + s, NLAT)
        return remote(x_ref.at[to // 2], col.at[lat], xs.at[s], xr.at[s], to, lon)

    def bcopy(s):
        to = lax.rem(lat + s, NLAT)
        return remote(o_s.at[to], back.at[lat], bs.at[s], br.at[s], to, lon)

    loop(1, NLAT, lambda s: xcopy(s).start())
    own = pltpu.make_async_copy(x_ref.at[lat // 2], col.at[lat], xr.at[0])
    own.start()
    own.wait()
    loop(1, NLAT, lambda s: xcopy(s).wait())
    x = col[...].reshape(512, D)
    qkv = lax.dot_general(
        w_ref[...], x, (((1,), (1,)), ((), ())), preferred_element_type=F32
    ).astype(BF)
    qkv_s[...] = qkv.reshape(24, HD, 512)

    def head(h):
        k_aug = jnp.concatenate([qkv_s[8 + h], ka_ref[...]], axis=0)
        q_aug = jnp.concatenate([qkv_s[h], qa_ref[...]], axis=0)
        v_aug = jnp.concatenate([qkv_s[16 + h], jnp.ones((16, 512), BF)], axis=0)
        t_s[h] = soft(k_aug, q_aug, v_aug)

    loop(0, 8, head)
    o = jnp.transpose(t_s[...].reshape(384, 512)).astype(BF)
    o_s[...] = o.reshape(NLAT, 16, 384)
    loop(1, NLAT, lambda s: bcopy(s).start())
    mine = pltpu.make_async_copy(o_s.at[lat], back.at[lat], br.at[0])
    mine.start()
    mine.wait()
    loop(1, NLAT, lambda s: bcopy(s).wait())


def lat_attend(x, w, ka, qa):
    return pl.pallas_call(
        lat_attend_kernel,
        out_shape=jax.ShapeDtypeStruct((NLAT, 16, 384), BF),
        in_specs=[VMEM, VMEM, VMEM, VMEM],
        out_specs=ANY,
        scratch_shapes=[
            pltpu.VMEM((NLAT, 16, D), BF),
            pltpu.VMEM((24, HD, 512), BF),
            pltpu.VMEM((8, HD, 512), F32),
            pltpu.VMEM((NLAT, 16, 384), BF),
            DMA((NLAT,)), DMA((NLAT,)), DMA((NLAT,)), DMA((NLAT,)),
        ],
        compiler_params=pltpu.CompilerParams(
            collective_id=3, has_side_effects=True, vmem_limit_bytes=LIMIT
        ),
    )(x, w, ka, qa)


def local(
    tokens, source_id, valid, source_table, gain_lon, gain_lat, wqkv_lon, wout_lon, wqkv_lat, wout_lat
):
    rows, cols, width = tokens.shape
    onehot = (source_id[:, :, None] == jnp.arange(source_table.shape[0], dtype=jnp.int32)).astype(F32)
    start = tokens.astype(F32) + jnp.einsum(
        "rcs,sd->rcd", onehot, source_table, precision=lax.Precision.HIGHEST
    )
    lat, lon = where_am_i()
    shard = jnp.concatenate([wqkv_lon, wout_lon, wqkv_lat, wout_lat], axis=1)
    land, vlon, vlat = gather_lat(shard, jnp.pad(valid, ((0, 4), (0, 64))))
    units = land.reshape(D, 384).T.reshape(8, HD, D)
    keep = lax.dynamic_index_in_dim(vlon, lon // 4, 1, keepdims=False)[:, :64]
    keep = keep.reshape(4, 4, 64).transpose(1, 0, 2).reshape(1, 1024)
    ka1 = jnp.pad(jnp.where(keep > 0, 0.0, -1e30).astype(BF), ((0, 15), (0, 0)))
    qa1 = jnp.pad(jnp.ones((1, 1024), BF), ((0, 15), (0, 0)))[:, :256]

    xn = normalize(start, gain_lon)
    row, u1 = lon_in(xn, units)
    land1, wo1, u2, wo2 = lon_attend(row.reshape(1024, D), u1.reshape(576, D), ka1, qa1, units)
    heads = land1.reshape(4, 4, 64, 256)[..., :192].transpose(0, 2, 1, 3).reshape(rows * cols, width)
    middle = start + lax.dot_general(
        heads, wo1.reshape(D, D), (((1,), (1,)), ((), ())), preferred_element_type=F32
    ).reshape(rows, cols, width)

    xn2 = normalize(middle, gain_lat).reshape(4, 16, 4, D).transpose(1, 0, 2, 3).reshape(16, 16, D)
    keep2 = lax.dynamic_slice_in_dim(vlat[:, :4, :], (lat // 2) * 4, 4, 2).reshape(1, 512)
    column = lax.broadcasted_iota(jnp.int32, (4, 512), 1) % 4
    same = column == lax.broadcasted_iota(jnp.int32, (4, 512), 0)
    ka2 = jnp.concatenate(
        [jnp.where(keep2 > 0, 0.0, -1e30), same.astype(F32), jnp.zeros((11, 512), F32)], axis=0
    ).astype(BF)
    qa2 = jnp.concatenate(
        [jnp.ones((1, 512), F32), jnp.where(same, 0.0, -1e34), jnp.zeros((11, 512), F32)], axis=0
    ).astype(BF)
    back = lat_attend(xn2, u2.reshape(1152, D), ka2, qa2)
    heads2 = back.reshape(16, 2, 4, 4, 384).transpose(2, 0, 3, 1, 4).reshape(rows * cols, width)
    branch = lax.dot_general(
        heads2, wo2.reshape(D, D), (((1,), (1,)), ((), ())), preferred_element_type=F32
    ).reshape(rows, cols, width)
    return (middle + branch).astype(BF)


def solution(mesh):
    placed = (
        P("lat", "lon", None),
        P("lat", "lon"),
        P("lat", "lon"),
        P(),
        P(),
        P(),
        P("lat", "lon"),
        P("lat", "lon"),
        P("lat", "lon"),
        P("lat", "lon"),
    )
    return jax.shard_map(
        local, mesh=mesh, in_specs=placed, out_specs=P("lat", "lon", None), check_vma=False
    )
```

```python
import functools

import jax
import jax.numpy as jnp
from jax import lax
from jax.experimental import pallas as pl
from jax.experimental.pallas import tpu as pltpu
from jax.sharding import PartitionSpec as P

HEADS = 16
HD = 48
D = 768
NLAT = 32
NLON = 16
MESH = pl.DeviceIdType.MESH
BF = jnp.bfloat16
F32 = jnp.float32
VMEM = pl.BlockSpec(memory_space=pltpu.VMEM)
DMA = pltpu.SemaphoreType.DMA
SCALE2 = float(1.4426950408889634 / (48.0**0.5))
LIMIT = 56 * 1024 * 1024


def normalize(x, gain):
    scale = lax.rsqrt(jnp.mean(x * x, axis=-1, keepdims=True) + 1e-06)
    return (x * scale * gain).astype(BF)


def nt(x, y):
    return lax.dot_general(x, y, (((1,), (1,)), ((), ())), preferred_element_type=F32)


def where_am_i():
    return lax.axis_index("lat"), lax.axis_index("lon")


def remote(src, dst, send, recv, lat, lon):
    return pltpu.make_async_remote_copy(
        src_ref=src,
        dst_ref=dst,
        send_sem=send,
        recv_sem=recv,
        device_id=(lat, lon),
        device_id_type=MESH,
    )


def shifted(lat, lon, t, sign):
    core = lax.rem(lat, 2)
    dyi = t // 4
    off = dyi + 4 * (dyi // 3) + 4 * core * ((dyi // 2) * (3 - dyi))
    y = (lat // 16) * 4 + lon // 4
    y2 = lax.rem(y + off, 8) if sign > 0 else lax.rem(y + 8 - off, 8)
    dx = lax.rem(t, 4)
    x = lax.rem(lon, 4)
    x2 = lax.rem(x + dx, 4) if sign > 0 else lax.rem(x + 4 - dx, 4)
    return lax.rem(lat, 16) + 16 * (y2 // 4), lax.rem(y2, 4) * 4 + x2


def signal(sem, lat, lon):
    pl.semaphore_signal(sem, inc=1, device_id=(lat, lon), device_id_type=MESH)


def loop(lo, hi, body):
    def step(i, carry):
        body(i)
        return carry

    lax.fori_loop(lo, hi, step, 0)


def head_unit(lon, i):
    u = lon * 3 + i
    return u // 16, lax.rem(u, 16)


def soft(k_aug, q_aug, v_aug):
    s = lax.dot_general(k_aug, q_aug, (((0,), (0,)), ((), ())), preferred_element_type=F32)
    m = jnp.max(s, axis=0, keepdims=True)
    p = jnp.exp2((s - m) * SCALE2).astype(BF)
    o = jnp.dot(v_aug, p, preferred_element_type=F32)
    return o[:HD] / o[HD : HD + 1]


def arrived(ref, sem):
    return pltpu.make_async_copy(ref, ref, sem)


def pair_kernel(
    shard, tok, sid, table, g1, g2, v1, v2, e_ref, qa1, ka2c, qa2, out,
    land, units, start_s, xn_s, row, u1, wo1, u2, wo2, vl, mv, q_s, kv_s, t_s, o_s, land_o,
    x2_s, col, qkv2, t2, o2_s, back,
    s1s, s1r, sbs, sbr, v1s, v1r, v2s, v2r, ys, xs, rr, u1s, u1r, u1f, w1s, w1r, w1f, u2s, u2r,
    w2s, w2r, w2f, os, orr, x2s, x2r, x2f, bs, br,
):
    lat, lon = where_am_i()
    a, b = lon // 4, lax.rem(lon, 4)
    core, place = lax.rem(lat, 2), lat // 2
    sib = lat + 1 - 2 * core

    bar = pltpu.get_barrier_semaphore()
    loop(1, NLAT, lambda s: signal(bar, lax.rem(lat + s, NLAT), lon))

    def greet(t):
        p, q = shifted(lat, lon, t, -1)
        signal(bar, p, q)
        signal(bar, lat, lax.rem(lon + t, NLON))

    loop(1, 16, greet)
    pl.semaphore_wait(bar, 61)

    def wcopy(s):
        to = lax.rem(place + s, 16)
        return remote(shard, land.at[core, place], s1s.at[s], s1r.at[place], to * 2 + core, lon)

    loop(1, 16, lambda s: wcopy(s).start())
    land[core, place] = shard[...]

    kind = lax.broadcasted_iota(jnp.int32, (8, 256), 0)
    onehot = jnp.where(kind == sid[...], 1.0, 0.0)
    emb = lax.dot_general(
        onehot, table[...], (((0,), (0,)), ((), ())),
        precision=lax.Precision.HIGHEST, preferred_element_type=F32,
    )
    start = tok[...].astype(F32) + emb
    start_s[...] = start
    xn_s[...] = normalize(start, g1[...]).reshape(4, 64, D)

    def ycopy(s):
        to = lax.rem(a + s, 4)
        return remote(xn_s.at[to], row.at[b, a], ys.at[s], rr.at[b, a], lat, to * 4 + b)

    def xcopy(s, aa):
        to = lax.rem(b + s, 4)
        return remote(row.at[b, aa], row.at[b, aa], xs.at[s, aa], rr.at[b, aa], lat, a * 4 + to)

    loop(1, 4, lambda s: ycopy(s).start())
    row[b, a] = xn_s[a]
    loop(1, 4, lambda s: xcopy(s, a).start())

    def v1copy(s):
        to = lax.rem(lon + s, NLON)
        return remote(v1.at[to // 4], vl.at[lon], v1s.at[s], v1r.at[lon], lat, to)

    def v2copy(s):
        to = lax.rem(lat + s, NLAT)
        return remote(v2.at[to // 2], mv.at[core, place], v2s.at[s], v2r.at[core, place], to, lon)

    loop(1, 16, lambda s: v1copy(s).start())
    loop(1, NLAT, lambda s: v2copy(s).start())
    vl[lon] = v1[a]
    mv[core, place] = v2[place]

    def missing(s):
        src = lax.rem(place + 16 - s, 16)
        arrived(land.at[core, src], s1r.at[src]).wait()

    loop(1, 16, missing)
    sibling = remote(land.at[core], land.at[core], sbs, sbr, sib, lon)
    sibling.start()

    def forward(s):
        src = lax.rem(a + 4 - s, 4)
        arrived(row.at[b, src], rr.at[b, src]).wait()
        loop(1, 4, lambda k: xcopy(k, src).start())

    loop(1, 4, forward)
    arrived(land.at[1 - core], sbr).wait()

    w = land[...].astype(F32)
    w = jnp.stack([w[0], w[1]], axis=1).reshape(D, 384)
    units[...] = jnp.transpose(w).astype(BF).reshape(8, HD, D)

    def each_u1(act):
        for i in range(3):
            part, h = head_unit(lon, i)
            slot = part * 4 + lax.rem(h, 4)
            g = h // 4

            @pl.when(lax.rem(h, 2) == core)
            def _():
                def dest(dyi):
                    t = dyi * 4 + lax.rem(g - b + 4, 4)
                    p, q = shifted(lat, lon, t, 1)
                    far = remote(units.at[i], u1.at[slot], u1s.at[i, dyi], u1r.at[slot], p, q)

                    @pl.when(t == 0)
                    def _():
                        if act == "start":
                            pltpu.make_async_copy(units.at[i], u1.at[slot], u1r.at[slot]).start()

                    @pl.when(t != 0)
                    def _():
                        if act == "start":
                            far.start()
                        else:
                            far.wait_send()

                loop(0, 4, dest)

    each_u1("start")

    def wcast(unit, dst, ssem, rsem):
        def one(t):
            p, q = shifted(lat, lon, t, 1)
            return remote(units.at[unit], dst.at[lon], ssem.at[t], rsem.at[lon], p, q)

        return one

    wo1copy = wcast(3, wo1, w1s, w1r)
    wo2copy = wcast(7, wo2, w2s, w2r)
    sends = lax.rem(lon, 2) == core

    def wbegin(copy, unit, dst, rsem):
        @pl.when(sends)
        def _():
            loop(1, 16, lambda t: copy(t).start())
            pltpu.make_async_copy(units.at[unit], dst.at[lon], rsem.at[lon]).start()

    def wshare(dst, rsem, fsem, k):
        slot = 2 * k + core
        return remote(dst.at[slot], dst.at[slot], fsem.at[k], rsem.at[slot], sib, lon)

    def wforward(dst, rsem, fsem):
        def one(k):
            arrived(dst.at[2 * k + core], rsem.at[2 * k + core]).wait()
            wshare(dst, rsem, fsem, k).start()

        loop(0, 8, one)

    def wrest(dst, rsem):
        loop(0, 8, lambda k: arrived(dst.at[2 * k + 1 - core], rsem.at[2 * k + 1 - core]).wait())

    def u2do(act):
        for i in range(3):
            part, h = head_unit(lon, i)
            slot = part * 8 + lax.rem(h, 8)

            @pl.when(h // 8 == core)
            def _():
                def one(t):
                    p, q = shifted(lat, lon, t, 1)
                    c = remote(units.at[4 + i], u2.at[slot], u2s.at[i, t], u2r.at[slot], p, q)
                    if act == "start":
                        c.start()
                    else:
                        c.wait_send()

                loop(1, 16, one)
                if act == "start":
                    pltpu.make_async_copy(units.at[4 + i], u2.at[slot], u2r.at[slot]).start()

    def u1slot(k, c):
        return (k // 2) * 4 + lax.rem(k, 2) * 2 + c

    def u1share(k):
        slot = u1slot(k, core)
        return remote(u1.at[slot], u1.at[slot], u1f.at[k], u1r.at[slot], sib, lon)

    def u1forward(k):
        slot = u1slot(k, core)
        arrived(u1.at[slot], u1r.at[slot]).wait()
        u1share(k).start()

    loop(0, 6, u1forward)
    wbegin(wo1copy, 3, wo1, w1r)
    loop(1, 16, lambda s: arrived(vl.at[lax.rem(lon + s, 16)], v1r.at[lax.rem(lon + s, 16)]).wait())

    def collect(s):
        src = lax.rem(b + s, 4)
        loop(0, 4, lambda aa: arrived(row.at[src, aa], rr.at[src, aa]).wait())

    loop(1, 4, collect)
    loop(0, 6, lambda k: arrived(u1.at[u1slot(k, 1 - core)], u1r.at[u1slot(k, 1 - core)]).wait())
    u2do("start")

    qkv = nt(u1[...].reshape(576, D), row[...].reshape(1024, D)).astype(BF)
    for h in range(4):
        for qb in range(4):
            q_s[qb, h] = qkv[h * HD : (h + 1) * HD, qb * 256 : (qb + 1) * 256]
        kv_s[h] = qkv[192 + h * HD : 192 + (h + 1) * HD]
        kv_s[4 + h] = qkv[384 + h * HD : 384 + (h + 1) * HD]
    ka1 = jnp.concatenate(
        [vl[(2 * (j % 2)) * 4 + j // 2] + vl[(2 * (j % 2) + 1) * 4 + j // 2] for j in range(8)], axis=1
    )
    o_s[...] = jnp.zeros_like(o_s)

    def ocopy(bb, aa):
        return remote(o_s.at[bb, aa], land_o.at[lon], os.at[bb, aa], orr.at[lon], lat, aa * 4 + bb)

    def block(qb):
        def head(h):
            k_aug = jnp.concatenate([kv_s[h], ka1], axis=0)
            q_aug = jnp.concatenate([q_s[qb, h], qa1[...]], axis=0)
            v_aug = jnp.concatenate([kv_s[4 + h], jnp.ones((16, 1024), BF)], axis=0)
            t_s[h] = soft(k_aug, q_aug, v_aug)

        loop(0, 4, head)
        o = jnp.transpose(t_s[...].reshape(192, 256)).astype(BF)
        for aa in range(4):
            o_s[qb, aa, :, :192] = o[aa * 64 : (aa + 1) * 64]

        def send(aa):
            @pl.when(aa * 4 + qb != lon)
            def _():
                ocopy(qb, aa).start()

        loop(0, 4, send)

    loop(0, 4, block)
    land_o[lon] = o_s[b, a]
    wbegin(wo2copy, 7, wo2, w2r)
    wforward(wo1, w1r, w1f)
    loop(1, 16, lambda s: arrived(land_o.at[lax.rem(lon + s, 16)], orr.at[lax.rem(lon + s, 16)]).wait())
    wrest(wo1, w1r)

    heads = jnp.concatenate(
        [
            jnp.concatenate([land_o[4 * k + g][:, :192] for g in range(4)], axis=1)
            for k in range(4)
        ],
        axis=0,
    )
    middle = start_s[...] + nt(heads, wo1[...].reshape(D, D))
    start_s[...] = middle

    i = lax.broadcasted_iota(jnp.int32, (256, 256), 0)
    j = lax.broadcasted_iota(jnp.int32, (256, 256), 1)
    from_row = ((i >> 2) & 3) * 64 + (i >> 4) * 4 + (i & 3)
    perm = jnp.where(from_row == j, 1.0, 0.0).astype(BF)
    xn2 = jnp.dot(perm, normalize(middle, g2[...]), preferred_element_type=F32).astype(BF)
    x2_s[...] = xn2.reshape(16, 16, D)

    def x2copy(s):
        to = lax.rem(place + s, 16)
        return remote(
            x2_s.at[to], col.at[core, place], x2s.at[s], x2r.at[core, place], to * 2 + core, lon
        )

    def x2share(src):
        return remote(col.at[core, src], col.at[core, src], x2f.at[src], x2r.at[core, src], sib, lon)

    loop(1, 16, lambda s: x2copy(s).start())
    col[core, place] = x2_s[place]
    x2share(place).start()

    def x2forward(s):
        src = lax.rem(place + 16 - s, 16)
        arrived(col.at[core, src], x2r.at[core, src]).wait()
        x2share(src).start()

    loop(1, 16, x2forward)

    def mwait(s):
        src = lax.rem(lat + NLAT - s, NLAT)
        c, p = lax.rem(src, 2), src // 2
        arrived(mv.at[c, p], v2r.at[c, p]).wait()

    loop(1, NLAT, mwait)
    loop(0, 24, lambda k: arrived(u2.at[k], u2r.at[k]).wait())
    loop(0, 16, lambda k: arrived(col.at[1 - core, k], x2r.at[1 - core, k]).wait())

    qkv2[...] = nt(u2[...].reshape(1152, D), col[...].reshape(512, D)).astype(BF).reshape(24, HD, 512)
    ka2 = (nt(e_ref[...], mv[...].reshape(512, 128)) + ka2c[...]).astype(BF)

    def head2(h):
        k_aug = jnp.concatenate([qkv2[8 + h], ka2], axis=0)
        q_aug = jnp.concatenate([qkv2[h], qa2[...]], axis=0)
        v_aug = jnp.concatenate([qkv2[16 + h], jnp.ones((16, 512), BF)], axis=0)
        t2[h] = soft(k_aug, q_aug, v_aug)

    loop(0, 8, head2)
    o2_s[...] = jnp.transpose(t2[...].reshape(384, 512)).astype(BF).reshape(2, 16, 16, 384)

    def bcopy(s):
        to = lax.rem(lat + s, NLAT)
        return remote(
            o2_s.at[lax.rem(to, 2), to // 2], back.at[core, place], bs.at[s], br.at[core, place], to, lon
        )

    loop(1, NLAT, lambda s: bcopy(s).start())
    back[core, place] = o2_s[core, place]
    wforward(wo2, w2r, w2f)

    def bwait(s):
        src = lax.rem(lat + NLAT - s, NLAT)
        c, p = lax.rem(src, 2), src // 2
        arrived(back.at[c, p], br.at[c, p]).wait()

    loop(1, NLAT, bwait)
    wrest(wo2, w2r)
    heads2 = jnp.concatenate([back[0].reshape(256, 384), back[1].reshape(256, 384)], axis=1)
    heads2 = lax.dot_general(
        perm, heads2, (((0,), (0,)), ((), ())), preferred_element_type=F32
    ).astype(BF)
    out[...] = (start_s[...] + nt(heads2, wo2[...].reshape(D, D))).astype(BF)

    loop(1, 16, lambda s: wcopy(s).wait_send())
    sibling.wait_send()
    loop(1, 16, lambda s: v1copy(s).wait_send())
    loop(1, NLAT, lambda s: v2copy(s).wait_send())
    loop(1, 4, lambda s: ycopy(s).wait_send())
    loop(1, 4, lambda s: loop(0, 4, lambda aa: xcopy(s, aa).wait_send()))
    each_u1("finish")
    loop(0, 6, lambda k: u1share(k).wait_send())

    @pl.when(sends)
    def _():
        loop(1, 16, lambda t: wo1copy(t).wait_send())
        loop(1, 16, lambda t: wo2copy(t).wait_send())

    loop(0, 8, lambda k: wshare(wo1, w1r, w1f, k).wait_send())
    loop(0, 8, lambda k: wshare(wo2, w2r, w2f, k).wait_send())
    u2do("finish")

    def osent(k):
        bb, aa = lax.rem(k, 4), k // 4

        @pl.when(k != lon)
        def _():
            ocopy(bb, aa).wait_send()

    loop(0, 16, osent)
    loop(1, 16, lambda s: x2copy(s).wait_send())
    loop(0, 16, lambda k: x2share(k).wait_send())
    loop(1, NLAT, lambda s: bcopy(s).wait_send())


def pair(*args):
    return pl.pallas_call(
        pair_kernel,
        out_shape=jax.ShapeDtypeStruct((256, D), BF),
        in_specs=[VMEM] * len(args),
        out_specs=VMEM,
        scratch_shapes=[
            pltpu.VMEM((2, 16, 24, 384), BF),
            pltpu.VMEM((8, HD, D), BF),
            pltpu.VMEM((256, D), F32),
            pltpu.VMEM((4, 64, D), BF),
            pltpu.VMEM((4, 4, 64, D), BF),
            pltpu.VMEM((12, HD, D), BF),
            pltpu.VMEM((16, HD, D), BF),
            pltpu.VMEM((24, HD, D), BF),
            pltpu.VMEM((16, HD, D), BF),
            pltpu.VMEM((16, 16, 128), BF),
            pltpu.VMEM((2, 16, 16, 128), BF),
            pltpu.VMEM((4, 4, HD, 256), BF),
            pltpu.VMEM((8, HD, 1024), BF),
            pltpu.VMEM((4, HD, 256), F32),
            pltpu.VMEM((4, 4, 64, 256), BF),
            pltpu.VMEM((16, 64, 256), BF),
            pltpu.VMEM((16, 16, D), BF),
            pltpu.VMEM((2, 16, 16, D), BF),
            pltpu.VMEM((24, HD, 512), BF),
            pltpu.VMEM((8, HD, 512), F32),
            pltpu.VMEM((2, 16, 16, 384), BF),
            pltpu.VMEM((2, 16, 16, 384), BF),
            DMA((16,)), DMA((16,)), DMA, DMA, DMA((16,)), DMA((16,)), DMA((NLAT,)), DMA((2, 16)),
            DMA((4,)), DMA((4, 4)), DMA((4, 4)), DMA((3, 4)), DMA((12,)), DMA((6,)),
            DMA((16,)), DMA((16,)), DMA((8,)), DMA((3, 16)), DMA((24,)),
            DMA((16,)), DMA((16,)), DMA((8,)), DMA((4, 4)), DMA((16,)),
            DMA((16,)), DMA((2, 16)), DMA((16,)), DMA((NLAT,)), DMA((2, 16)),
        ],
        compiler_params=pltpu.CompilerParams(
            collective_id=0, has_side_effects=True, vmem_limit_bytes=LIMIT
        ),
    )(*args)


def local(
    tokens, source_id, valid, source_table, gain_lon, gain_lat, wqkv_lon, wout_lon, wqkv_lat, wout_lat
):
    rows, cols, width = tokens.shape
    lat, lon = where_am_i()
    shard = jnp.concatenate([wqkv_lon, wout_lon, wqkv_lat, wout_lat], axis=1)
    bias = jnp.where(valid > 0, 0.0, -1e30).astype(BF)
    low = jnp.pad(bias, ((0, 0), (0, 64)))
    high = jnp.pad(bias, ((0, 0), (64, 0)))
    v1 = jnp.where((lon // 4) % 2 == 0, low, high)[:, None, :]
    v1 = jnp.pad(v1, ((0, 0), (0, 15), (0, 0)))
    v2 = bias.reshape(4, 16, 4).transpose(1, 0, 2).reshape(16, 16, 1)
    v2 = jnp.pad(v2, ((0, 0), (0, 0), (0, 127)))
    e = jnp.zeros((16, 128), F32).at[0, 0].set(1.0).astype(BF)
    qa1 = jnp.zeros((16, 256), F32).at[0].set(1.0).astype(BF)
    r = lax.broadcasted_iota(jnp.int32, (16, 512), 0)
    same = (lax.broadcasted_iota(jnp.int32, (16, 512), 1) % 4) == r - 1
    column = (r >= 1) & (r <= 4)
    ka2 = jnp.where(same, 1.0, 0.0)
    qa2 = jnp.where(r == 0, 1.0, jnp.where(column & ~same, -1e34, 0.0)).astype(BF)
    mixed = pair(
        shard,
        tokens.reshape(rows * cols, width),
        source_id.reshape(1, rows * cols),
        jnp.pad(source_table, ((0, 3), (0, 0))),
        gain_lon.reshape(1, width),
        gain_lat.reshape(1, width),
        v1,
        v2,
        e,
        qa1,
        ka2,
        qa2,
    )
    return mixed.reshape(rows, cols, width)


def solution(mesh):
    placed = (
        P("lat", "lon", None),
        P("lat", "lon"),
        P("lat", "lon"),
        P(),
        P(),
        P(),
        P("lat", "lon"),
        P("lat", "lon"),
        P("lat", "lon"),
        P("lat", "lon"),
    )
    return jax.shard_map(
        local, mesh=mesh, in_specs=placed, out_specs=P("lat", "lon", None), check_vma=False
    )
```

```python
import functools

import jax
import jax.numpy as jnp
from jax import lax
from jax.experimental import pallas as pl
from jax.experimental.pallas import tpu as pltpu
from jax.sharding import PartitionSpec as P

HEADS = 16
HD = 48
D = 768
NLAT = 32
NLON = 16
MESH = pl.DeviceIdType.MESH
BF = jnp.bfloat16
F32 = jnp.float32
VMEM = pl.BlockSpec(memory_space=pltpu.VMEM)
DMA = pltpu.SemaphoreType.DMA
SCALE2 = float(1.4426950408889634 / (48.0**0.5))
LIMIT = 56 * 1024 * 1024


def normalize(x, gain):
    scale = lax.rsqrt(jnp.mean(x * x, axis=-1, keepdims=True) + 1e-06)
    return (x * scale * gain).astype(BF)


def nt(x, y):
    return lax.dot_general(x, y, (((1,), (1,)), ((), ())), preferred_element_type=F32)


def where_am_i():
    return lax.axis_index("lat"), lax.axis_index("lon")


def remote(src, dst, send, recv, lat, lon):
    return pltpu.make_async_remote_copy(
        src_ref=src,
        dst_ref=dst,
        send_sem=send,
        recv_sem=recv,
        device_id=(lat, lon),
        device_id_type=MESH,
    )


def shifted(lat, lon, t, sign):
    core = lax.rem(lat, 2)
    dyi = t // 4
    off = dyi + 4 * (dyi // 3) + 4 * core * ((dyi // 2) * (3 - dyi))
    y = (lat // 16) * 4 + lon // 4
    y2 = lax.rem(y + off, 8) if sign > 0 else lax.rem(y + 8 - off, 8)
    dx = lax.rem(t, 4)
    x = lax.rem(lon, 4)
    x2 = lax.rem(x + dx, 4) if sign > 0 else lax.rem(x + 4 - dx, 4)
    return lax.rem(lat, 16) + 16 * (y2 // 4), lax.rem(y2, 4) * 4 + x2


def signal(sem, lat, lon):
    pl.semaphore_signal(sem, inc=1, device_id=(lat, lon), device_id_type=MESH)


def loop(lo, hi, body):
    def step(i, carry):
        body(i)
        return carry

    lax.fori_loop(lo, hi, step, 0)


def head_unit(lon, i):
    u = lon * 3 + i
    return u // 16, lax.rem(u, 16)


def soft(k_aug, q_aug, v_aug):
    s = lax.dot_general(k_aug, q_aug, (((0,), (0,)), ((), ())), preferred_element_type=F32)
    m = jnp.max(s, axis=0, keepdims=True)
    p = jnp.exp2((s - m) * SCALE2).astype(BF)
    o = jnp.dot(v_aug, p, preferred_element_type=F32)
    return o[:HD] / o[HD : HD + 1]


def iota(shape, axis):
    return lax.broadcasted_iota(jnp.int32, shape, axis)


def arrived(ref, sem):
    return pltpu.make_async_copy(ref, ref, sem)


def pair_kernel(
    tok, sid, valid, table, g1, g2, wq1, wp1, wq2, wp2, out,
    shard, table_s, v1, v2,
    land, units, start_s, xn_s, row, u1, wo1, u2, wo2, vl, mv, q_s, kv_s, t_s, o_s, land_o,
    x2_s, col, qkv2, t2, o2_s, back,
    s1s, s1r, sbs, sbr, v1s, v1r, v2s, v2r, ys, xs, rr, u1s, u1r, u1f, w1s, w1r, w1f, u2s, u2r,
    u2f, w2s, w2r, w2f, os, orr, x2s, x2r, x2f, bs, br,
):
    lat, lon = where_am_i()
    a, b = lon // 4, lax.rem(lon, 4)
    core, place = lax.rem(lat, 2), lat // 2
    sib = lat + 1 - 2 * core

    bar = pltpu.get_barrier_semaphore()
    loop(1, NLAT, lambda s: signal(bar, lax.rem(lat + s, NLAT), lon))

    def greet(t):
        p, q = shifted(lat, lon, t, -1)
        signal(bar, p, q)
        signal(bar, lat, lax.rem(lon + t, NLON))

    loop(1, 16, greet)

    shard[...] = jnp.concatenate(
        [w[...].astype(F32) for w in (wq1, wp1, wq2, wp2)], axis=1
    ).astype(BF)
    table_s[...] = jnp.zeros_like(table_s)
    table_s[0:5] = table[...]
    ids = sid[...]
    bias = jnp.where(valid[...] > 0, 0.0, -1e30)
    for k in range(4):
        onehot = jnp.where(iota((8, 64), 0) == ids[k : k + 1], 1.0, 0.0)
        emb = lax.dot_general(
            onehot, table_s[...], (((0,), (0,)), ((), ())),
            precision=lax.Precision.HIGHEST, preferred_element_type=F32,
        )
        first = tok[k].astype(F32) + emb
        start_s[k * 64 : (k + 1) * 64] = first
        xn_s[k] = normalize(first, g1[...].reshape(1, D))
        line = jnp.where(iota((16, 64), 0) == 0, bias[k : k + 1], 0.0)
        none = jnp.zeros((16, 64), F32)
        v1[k] = jnp.where(
            lax.rem(a, 2) == 0,
            jnp.concatenate([line, none], axis=1),
            jnp.concatenate([none, line], axis=1),
        ).astype(BF)
    token, lane = iota((256, 64), 0), iota((256, 64), 1)
    picks = jnp.where((token >> 4) * 4 + (token & 3) == lane, 1.0, 0.0).astype(BF)
    tall = jnp.concatenate([bias, jnp.zeros((124, 64), F32)], axis=0).astype(BF)
    v2all = nt(picks, tall)
    v2all = jnp.where(iota((256, 128), 1) == ((iota((256, 128), 0) >> 2) & 3), v2all, 0.0)
    v2[...] = v2all.astype(BF).reshape(16, 16, 128)

    pl.semaphore_wait(bar, 61)

    def wcopy(s):
        to = lax.rem(place + s, 16)
        return remote(shard, land.at[core, place], s1s.at[s], s1r.at[place], to * 2 + core, lon)

    loop(1, 16, lambda s: wcopy(s).start())
    land[core, place] = shard[...]


    def ycopy(s):
        to = lax.rem(a + s, 4)
        return remote(xn_s.at[to], row.at[b, a], ys.at[s], rr.at[b, a], lat, to * 4 + b)

    def xcopy(s, aa):
        to = lax.rem(b + s, 4)
        return remote(row.at[b, aa], row.at[b, aa], xs.at[s, aa], rr.at[b, aa], lat, a * 4 + to)

    loop(1, 4, lambda s: ycopy(s).start())
    row[b, a] = xn_s[a]
    loop(1, 4, lambda s: xcopy(s, a).start())

    def v1copy(s):
        to = lax.rem(lon + s, NLON)
        return remote(v1.at[to // 4], vl.at[lon], v1s.at[s], v1r.at[lon], lat, to)

    def v2copy(s):
        to = lax.rem(lat + s, NLAT)
        return remote(v2.at[to // 2], mv.at[core, place], v2s.at[s], v2r.at[core, place], to, lon)

    loop(1, 16, lambda s: v1copy(s).start())
    loop(1, NLAT, lambda s: v2copy(s).start())
    vl[lon] = v1[a]
    mv[core, place] = v2[place]

    def missing(s):
        src = lax.rem(place + 16 - s, 16)
        arrived(land.at[core, src], s1r.at[src]).wait()

    loop(1, 16, missing)
    sibling = remote(land.at[core], land.at[core], sbs, sbr, sib, lon)
    sibling.start()

    def forward(s):
        src = lax.rem(a + 4 - s, 4)
        arrived(row.at[b, src], rr.at[b, src]).wait()
        loop(1, 4, lambda k: xcopy(k, src).start())

    loop(1, 4, forward)
    arrived(land.at[1 - core], sbr).wait()

    w = land[...].astype(F32)
    w = jnp.stack([w[0], w[1]], axis=1).reshape(D, 384)
    units[...] = jnp.transpose(w).astype(BF).reshape(8, HD, D)

    def each_u1(act):
        for i in range(3):
            part, h = head_unit(lon, i)
            slot = part * 4 + lax.rem(h, 4)
            g = h // 4

            @pl.when(lax.rem(h, 2) == core)
            def _():
                def dest(dyi):
                    t = dyi * 4 + lax.rem(g - b + 4, 4)
                    p, q = shifted(lat, lon, t, 1)
                    far = remote(units.at[i], u1.at[slot], u1s.at[i, dyi], u1r.at[slot], p, q)

                    @pl.when(t == 0)
                    def _():
                        if act == "start":
                            pltpu.make_async_copy(units.at[i], u1.at[slot], u1r.at[slot]).start()

                    @pl.when(t != 0)
                    def _():
                        if act == "start":
                            far.start()
                        else:
                            far.wait_send()

                loop(0, 4, dest)

    each_u1("start")

    def wcast(unit, dst, ssem, rsem):
        def one(t):
            p, q = shifted(lat, lon, t, 1)
            return remote(units.at[unit], dst.at[lon], ssem.at[t], rsem.at[lon], p, q)

        return one

    wo1copy = wcast(3, wo1, w1s, w1r)
    wo2copy = wcast(7, wo2, w2s, w2r)
    sends = lax.rem(lon, 2) == core

    def wbegin(copy, unit, dst, rsem):
        @pl.when(sends)
        def _():
            loop(1, 16, lambda t: copy(t).start())
            pltpu.make_async_copy(units.at[unit], dst.at[lon], rsem.at[lon]).start()

    def wshare(dst, rsem, fsem, k):
        slot = 2 * k + core
        return remote(dst.at[slot], dst.at[slot], fsem.at[k], rsem.at[slot], sib, lon)

    def wforward(dst, rsem, fsem):
        def one(k):
            arrived(dst.at[2 * k + core], rsem.at[2 * k + core]).wait()
            wshare(dst, rsem, fsem, k).start()

        loop(0, 8, one)

    def wrest(dst, rsem):
        loop(0, 8, lambda k: arrived(dst.at[2 * k + 1 - core], rsem.at[2 * k + 1 - core]).wait())

    def u2do(act):
        for i in range(3):
            part, h = head_unit(lon, i)
            slot = part * 8 + lax.rem(h, 8)

            here = h // 8 == core
            here = here if i == 0 else here & (lax.rem(place, 2) == i - 1)

            @pl.when(here)
            def _():
                def one(t):
                    p, q = shifted(lat, lon, t, 1)
                    c = remote(units.at[4 + i], u2.at[slot], u2s.at[i, t], u2r.at[slot], p, q)
                    if act == "start":
                        c.start()
                    else:
                        c.wait_send()

                loop(1, 16, one)
                if act == "start":
                    pltpu.make_async_copy(units.at[4 + i], u2.at[slot], u2r.at[slot]).start()

    zsib = lat + 2 - 4 * lax.rem(place, 2)

    def u2class(k):
        return lax.rem((k // 8) * 16 + core * 8 + lax.rem(k, 8), 3)

    def u2share(k):
        return remote(u2.at[k], u2.at[k], u2f.at[k], u2r.at[k], zsib, lon)

    def u2pass(act):
        def one(k):
            @pl.when(u2class(k) == 1 + lax.rem(place, 2))
            def _():
                if act == "start":
                    arrived(u2.at[k], u2r.at[k]).wait()
                    u2share(k).start()
                else:
                    u2share(k).wait_send()

        loop(0, 24, one)

    def u2rest(k):
        @pl.when(u2class(k) != 1 + lax.rem(place, 2))
        def _():
            arrived(u2.at[k], u2r.at[k]).wait()

    def u1slot(k, c):
        return (k // 2) * 4 + lax.rem(k, 2) * 2 + c

    def u1share(k):
        slot = u1slot(k, core)
        return remote(u1.at[slot], u1.at[slot], u1f.at[k], u1r.at[slot], sib, lon)

    def u1forward(k):
        slot = u1slot(k, core)
        arrived(u1.at[slot], u1r.at[slot]).wait()
        u1share(k).start()

    loop(0, 6, u1forward)
    wbegin(wo1copy, 3, wo1, w1r)
    loop(1, 16, lambda s: arrived(vl.at[lax.rem(lon + s, 16)], v1r.at[lax.rem(lon + s, 16)]).wait())

    def collect(s):
        src = lax.rem(b + s, 4)
        loop(0, 4, lambda aa: arrived(row.at[src, aa], rr.at[src, aa]).wait())

    loop(1, 4, collect)
    loop(0, 6, lambda k: arrived(u1.at[u1slot(k, 1 - core)], u1r.at[u1slot(k, 1 - core)]).wait())
    u2do("start")

    qkv = nt(u1[...].reshape(576, D), row[...].reshape(1024, D)).astype(BF)
    for h in range(4):
        for qb in range(4):
            q_s[qb, h] = qkv[h * HD : (h + 1) * HD, qb * 256 : (qb + 1) * 256]
        kv_s[h] = qkv[192 + h * HD : 192 + (h + 1) * HD]
        kv_s[4 + h] = qkv[384 + h * HD : 384 + (h + 1) * HD]
    ka1 = jnp.concatenate(
        [vl[(2 * (j % 2)) * 4 + j // 2] + vl[(2 * (j % 2) + 1) * 4 + j // 2] for j in range(8)], axis=1
    )
    qa1 = jnp.where(iota((16, 256), 0) == 0, 1.0, 0.0).astype(BF)
    o_s[...] = jnp.zeros_like(o_s)

    def ocopy(bb, aa):
        return remote(o_s.at[bb, aa], land_o.at[lon], os.at[bb, aa], orr.at[lon], lat, aa * 4 + bb)

    def block(qb):
        def head(h):
            k_aug = jnp.concatenate([kv_s[h], ka1], axis=0)
            q_aug = jnp.concatenate([q_s[qb, h], qa1], axis=0)
            v_aug = jnp.concatenate([kv_s[4 + h], jnp.ones((16, 1024), BF)], axis=0)
            t_s[h] = soft(k_aug, q_aug, v_aug)

        loop(0, 4, head)
        o = jnp.transpose(t_s[...].reshape(192, 256)).astype(BF)
        for aa in range(4):
            o_s[qb, aa, :, :192] = o[aa * 64 : (aa + 1) * 64]

        def send(aa):
            @pl.when(aa * 4 + qb != lon)
            def _():
                ocopy(qb, aa).start()

        loop(0, 4, send)

    loop(0, 4, block)
    land_o[lon] = o_s[b, a]
    wforward(wo1, w1r, w1f)
    u2pass("start")
    loop(1, 16, lambda s: arrived(land_o.at[lax.rem(lon + s, 16)], orr.at[lax.rem(lon + s, 16)]).wait())
    wrest(wo1, w1r)

    heads = jnp.concatenate(
        [
            jnp.concatenate([land_o[4 * k + g][:, :192] for g in range(4)], axis=1)
            for k in range(4)
        ],
        axis=0,
    )
    middle = start_s[...] + nt(heads, wo1[...].reshape(D, D))
    start_s[...] = middle

    i = lax.broadcasted_iota(jnp.int32, (256, 256), 0)
    j = lax.broadcasted_iota(jnp.int32, (256, 256), 1)
    from_row = ((i >> 2) & 3) * 64 + (i >> 4) * 4 + (i & 3)
    perm = jnp.where(from_row == j, 1.0, 0.0).astype(BF)
    xn2 = jnp.dot(perm, normalize(middle, g2[...].reshape(1, D)), preferred_element_type=F32).astype(BF)
    x2_s[...] = xn2.reshape(16, 16, D)

    def x2copy(s):
        to = lax.rem(place + s, 16)
        return remote(
            x2_s.at[to], col.at[core, place], x2s.at[s], x2r.at[core, place], to * 2 + core, lon
        )

    def x2share(src):
        return remote(col.at[core, src], col.at[core, src], x2f.at[src], x2r.at[core, src], sib, lon)

    loop(1, 16, lambda s: x2copy(s).start())
    col[core, place] = x2_s[place]
    x2share(place).start()

    def x2forward(s):
        src = lax.rem(place + 16 - s, 16)
        arrived(col.at[core, src], x2r.at[core, src]).wait()
        x2share(src).start()

    loop(1, 16, x2forward)
    wbegin(wo2copy, 7, wo2, w2r)

    def mwait(s):
        src = lax.rem(lat + NLAT - s, NLAT)
        c, p = lax.rem(src, 2), src // 2
        arrived(mv.at[c, p], v2r.at[c, p]).wait()

    loop(1, NLAT, mwait)
    loop(0, 24, u2rest)
    loop(0, 16, lambda k: arrived(col.at[1 - core, k], x2r.at[1 - core, k]).wait())

    qkv2[...] = nt(u2[...].reshape(1152, D), col[...].reshape(512, D)).astype(BF).reshape(24, HD, 512)
    first = jnp.where((iota((16, 128), 0) == 0) & (iota((16, 128), 1) < 4), 1.0, 0.0).astype(BF)
    fr = iota((16, 512), 0)
    same = (iota((16, 512), 1) & 3) == fr - 1
    ka2 = (nt(first, mv[...].reshape(512, 128)) + jnp.where(same, 1.0, 0.0)).astype(BF)
    other = (fr >= 1) & (fr <= 4) & jnp.logical_not(same)
    qa2 = jnp.where(fr == 0, 1.0, jnp.where(other, -1e34, 0.0)).astype(BF)

    def head2(h):
        k_aug = jnp.concatenate([qkv2[8 + h], ka2], axis=0)
        q_aug = jnp.concatenate([qkv2[h], qa2], axis=0)
        v_aug = jnp.concatenate([qkv2[16 + h], jnp.ones((16, 512), BF)], axis=0)
        t2[h] = soft(k_aug, q_aug, v_aug)

    loop(0, 8, head2)
    o2_s[...] = jnp.transpose(t2[...].reshape(384, 512)).astype(BF).reshape(2, 16, 16, 384)

    def bcopy(s):
        to = lax.rem(lat + s, NLAT)
        return remote(
            o2_s.at[lax.rem(to, 2), to // 2], back.at[core, place], bs.at[s], br.at[core, place], to, lon
        )

    loop(1, NLAT, lambda s: bcopy(s).start())
    back[core, place] = o2_s[core, place]
    wforward(wo2, w2r, w2f)

    def bwait(s):
        src = lax.rem(lat + NLAT - s, NLAT)
        c, p = lax.rem(src, 2), src // 2
        arrived(back.at[c, p], br.at[c, p]).wait()

    loop(1, NLAT, bwait)
    wrest(wo2, w2r)
    heads2 = jnp.concatenate([back[0].reshape(256, 384), back[1].reshape(256, 384)], axis=1)
    heads2 = lax.dot_general(
        perm, heads2, (((0,), (0,)), ((), ())), preferred_element_type=F32
    ).astype(BF)
    out[...] = (start_s[...] + nt(heads2, wo2[...].reshape(D, D))).astype(BF).reshape(4, 64, D)

    loop(1, 16, lambda s: wcopy(s).wait_send())
    sibling.wait_send()
    loop(1, 16, lambda s: v1copy(s).wait_send())
    loop(1, NLAT, lambda s: v2copy(s).wait_send())
    loop(1, 4, lambda s: ycopy(s).wait_send())
    loop(1, 4, lambda s: loop(0, 4, lambda aa: xcopy(s, aa).wait_send()))
    each_u1("finish")
    loop(0, 6, lambda k: u1share(k).wait_send())

    @pl.when(sends)
    def _():
        loop(1, 16, lambda t: wo1copy(t).wait_send())
        loop(1, 16, lambda t: wo2copy(t).wait_send())

    loop(0, 8, lambda k: wshare(wo1, w1r, w1f, k).wait_send())
    loop(0, 8, lambda k: wshare(wo2, w2r, w2f, k).wait_send())
    u2do("finish")
    u2pass("finish")

    def osent(k):
        bb, aa = lax.rem(k, 4), k // 4

        @pl.when(k != lon)
        def _():
            ocopy(bb, aa).wait_send()

    loop(0, 16, osent)
    loop(1, 16, lambda s: x2copy(s).wait_send())
    loop(0, 16, lambda k: x2share(k).wait_send())
    loop(1, NLAT, lambda s: bcopy(s).wait_send())


def pair(*args):
    return pl.pallas_call(
        pair_kernel,
        out_shape=jax.ShapeDtypeStruct((4, 64, D), BF),
        in_specs=[VMEM] * len(args),
        out_specs=VMEM,
        scratch_shapes=[
            pltpu.VMEM((24, 384), BF),
            pltpu.VMEM((8, D), F32),
            pltpu.VMEM((4, 16, 128), BF),
            pltpu.VMEM((16, 16, 128), BF),
            pltpu.VMEM((2, 16, 24, 384), BF),
            pltpu.VMEM((8, HD, D), BF),
            pltpu.VMEM((256, D), F32),
            pltpu.VMEM((4, 64, D), BF),
            pltpu.VMEM((4, 4, 64, D), BF),
            pltpu.VMEM((12, HD, D), BF),
            pltpu.VMEM((16, HD, D), BF),
            pltpu.VMEM((24, HD, D), BF),
            pltpu.VMEM((16, HD, D), BF),
            pltpu.VMEM((16, 16, 128), BF),
            pltpu.VMEM((2, 16, 16, 128), BF),
            pltpu.VMEM((4, 4, HD, 256), BF),
            pltpu.VMEM((8, HD, 1024), BF),
            pltpu.VMEM((4, HD, 256), F32),
            pltpu.VMEM((4, 4, 64, 256), BF),
            pltpu.VMEM((16, 64, 256), BF),
            pltpu.VMEM((16, 16, D), BF),
            pltpu.VMEM((2, 16, 16, D), BF),
            pltpu.VMEM((24, HD, 512), BF),
            pltpu.VMEM((8, HD, 512), F32),
            pltpu.VMEM((2, 16, 16, 384), BF),
            pltpu.VMEM((2, 16, 16, 384), BF),
            DMA((16,)), DMA((16,)), DMA, DMA, DMA((16,)), DMA((16,)), DMA((NLAT,)), DMA((2, 16)),
            DMA((4,)), DMA((4, 4)), DMA((4, 4)), DMA((3, 4)), DMA((12,)), DMA((6,)),
            DMA((16,)), DMA((16,)), DMA((8,)), DMA((3, 16)), DMA((24,)), DMA((24,)),
            DMA((16,)), DMA((16,)), DMA((8,)), DMA((4, 4)), DMA((16,)),
            DMA((16,)), DMA((2, 16)), DMA((16,)), DMA((NLAT,)), DMA((2, 16)),
        ],
        compiler_params=pltpu.CompilerParams(
            collective_id=0, has_side_effects=True, vmem_limit_bytes=LIMIT
        ),
    )(*args)


def local(
    tokens, source_id, valid, source_table, gain_lon, gain_lat, wqkv_lon, wout_lon, wqkv_lat, wout_lat
):
    return pair(
        tokens, source_id, valid, source_table, gain_lon, gain_lat, wqkv_lon, wout_lon, wqkv_lat, wout_lat
    )


def solution(mesh):
    placed = (
        P("lat", "lon", None),
        P("lat", "lon"),
        P("lat", "lon"),
        P(),
        P(),
        P(),
        P("lat", "lon"),
        P("lat", "lon"),
        P("lat", "lon"),
        P("lat", "lon"),
    )
    return jax.shard_map(
        local, mesh=mesh, in_specs=placed, out_specs=P("lat", "lon", None), check_vma=False
    )
```

```python
import functools

import jax
import jax.numpy as jnp
from jax import lax
from jax.experimental import pallas as pl
from jax.experimental.pallas import tpu as pltpu
from jax.sharding import PartitionSpec as P

HEADS = 16
HD = 48
D = 768
NLAT = 32
NLON = 16
MESH = pl.DeviceIdType.MESH
BF = jnp.bfloat16
F32 = jnp.float32
VMEM = pl.BlockSpec(memory_space=pltpu.VMEM)
DMA = pltpu.SemaphoreType.DMA
SCALE2 = float(1.4426950408889634 / (48.0**0.5))
LIMIT = 56 * 1024 * 1024


def normalize(x, gain):
    scale = lax.rsqrt(jnp.mean(x * x, axis=-1, keepdims=True) + 1e-06)
    return (x * scale * gain).astype(BF)


def nt(x, y):
    return lax.dot_general(x, y, (((1,), (1,)), ((), ())), preferred_element_type=F32)


def where_am_i():
    return lax.axis_index("lat"), lax.axis_index("lon")


def remote(src, dst, send, recv, lat, lon):
    return pltpu.make_async_remote_copy(
        src_ref=src,
        dst_ref=dst,
        send_sem=send,
        recv_sem=recv,
        device_id=(lat, lon),
        device_id_type=MESH,
    )


def shifted(lat, lon, t, sign):
    core = lax.rem(lat, 2)
    dyi = t // 4
    off = dyi + 4 * (dyi // 3) + 4 * core * ((dyi // 2) * (3 - dyi))
    y = (lat // 16) * 4 + lon // 4
    y2 = lax.rem(y + off, 8) if sign > 0 else lax.rem(y + 8 - off, 8)
    dx = lax.rem(t, 4)
    x = lax.rem(lon, 4)
    x2 = lax.rem(x + dx, 4) if sign > 0 else lax.rem(x + 4 - dx, 4)
    return lax.rem(lat, 16) + 16 * (y2 // 4), lax.rem(y2, 4) * 4 + x2


def signal(sem, lat, lon):
    pl.semaphore_signal(sem, inc=1, device_id=(lat, lon), device_id_type=MESH)


def loop(lo, hi, body):
    def step(i, carry):
        body(i)
        return carry

    lax.fori_loop(lo, hi, step, 0)


def head_unit(lon, i):
    u = lon * 3 + i
    return u // 16, lax.rem(u, 16)


def soft(k_aug, q_aug, v_aug):
    s = lax.dot_general(k_aug, q_aug, (((0,), (0,)), ((), ())), preferred_element_type=F32)
    m = jnp.max(s, axis=0, keepdims=True)
    p = jnp.exp2((s - m) * SCALE2).astype(BF)
    o = jnp.dot(v_aug, p, preferred_element_type=F32)
    return o[:HD] / o[HD : HD + 1]


def iota(shape, axis):
    return lax.broadcasted_iota(jnp.int32, shape, axis)


def arrived(ref, sem):
    return pltpu.make_async_copy(ref, ref, sem)


def pair_kernel(
    tok, sid, valid, table, g1, g2, wq1, wp1, wq2, wp2, out,
    shard, table_s, v1, v2,
    land, units, start_s, xn_s, row, u1, wo1, u2, wo2, vl, mv, q_s, kv_s, t_s, o_s, land_o,
    x2_s, col, qkv2, t2, o2_s, back,
    s1s, s1r, sbs, sbr, v1s, v1r, v2s, v2r, ys, xs, rr, u1s, u1r, u1f, w1s, w1r, w1f, u2s, u2r,
    u2f, w2s, w2r, w2f, os, orr, x2s, x2r, x2f, bs, br,
):
    lat, lon = where_am_i()
    a, b = lon // 4, lax.rem(lon, 4)
    core, place = lax.rem(lat, 2), lat // 2
    sib = lat + 1 - 2 * core

    bar = pltpu.get_barrier_semaphore()
    loop(1, NLAT, lambda s: signal(bar, lax.rem(lat + s, NLAT), lon))

    def greet(t):
        p, q = shifted(lat, lon, t, -1)
        signal(bar, p, q)
        signal(bar, lat, lax.rem(lon + t, NLON))

    loop(1, 16, greet)

    shard[...] = jnp.concatenate(
        [w[...].astype(F32) for w in (wq1, wp1, wq2, wp2)], axis=1
    ).astype(BF)
    land[core, place] = shard[...]
    pl.semaphore_wait(bar, 61)

    def wcopy(s):
        to = lax.rem(place + s, 16)
        return remote(shard, land.at[core, place], s1s.at[s], s1r.at[place], to * 2 + core, lon)

    loop(1, 16, lambda s: wcopy(s).start())

    def ycopy(s):
        to = lax.rem(a + s, 4)
        return remote(xn_s.at[to], row.at[b, a], ys.at[s], rr.at[b, a], lat, to * 4 + b)

    def xcopy(s, aa):
        to = lax.rem(b + s, 4)
        return remote(row.at[b, aa], row.at[b, aa], xs.at[s, aa], rr.at[b, aa], lat, a * 4 + to)

    table_s[...] = jnp.zeros_like(table_s)
    table_s[0:5] = table[...]
    ids = sid[...]
    for k in range(4):
        onehot = jnp.where(iota((8, 64), 0) == ids[k : k + 1], 1.0, 0.0)
        emb = lax.dot_general(
            onehot, table_s[...], (((0,), (0,)), ((), ())),
            precision=lax.Precision.HIGHEST, preferred_element_type=F32,
        )
        first = tok[k].astype(F32) + emb
        start_s[k * 64 : (k + 1) * 64] = first
        xn_s[k] = normalize(first, g1[...].reshape(1, D))

    loop(1, 4, lambda s: ycopy(s).start())
    row[b, a] = xn_s[a]
    loop(1, 4, lambda s: xcopy(s, a).start())

    bias = jnp.where(valid[...] > 0, 0.0, -1e30)
    for k in range(4):
        line = jnp.where(iota((16, 64), 0) == 0, bias[k : k + 1], 0.0)
        none = jnp.zeros((16, 64), F32)
        v1[k] = jnp.where(
            lax.rem(a, 2) == 0,
            jnp.concatenate([line, none], axis=1),
            jnp.concatenate([none, line], axis=1),
        ).astype(BF)
    token, lane = iota((256, 64), 0), iota((256, 64), 1)
    picks = jnp.where((token >> 4) * 4 + (token & 3) == lane, 1.0, 0.0).astype(BF)
    tall = jnp.concatenate([bias, jnp.zeros((124, 64), F32)], axis=0).astype(BF)
    v2all = nt(picks, tall)
    v2all = jnp.where(iota((256, 128), 1) == ((iota((256, 128), 0) >> 2) & 3), v2all, 0.0)
    v2[...] = v2all.astype(BF).reshape(16, 16, 128)

    def v1copy(s):
        to = lax.rem(lon + s, NLON)
        return remote(v1.at[to // 4], vl.at[lon], v1s.at[s], v1r.at[lon], lat, to)

    def v2copy(s):
        to = lax.rem(lat + s, NLAT)
        return remote(v2.at[to // 2], mv.at[core, place], v2s.at[s], v2r.at[core, place], to, lon)

    loop(1, 16, lambda s: v1copy(s).start())
    loop(1, NLAT, lambda s: v2copy(s).start())
    vl[lon] = v1[a]
    mv[core, place] = v2[place]

    def missing(s):
        src = lax.rem(place + 16 - s, 16)
        arrived(land.at[core, src], s1r.at[src]).wait()

    loop(1, 16, missing)
    sibling = remote(land.at[core], land.at[core], sbs, sbr, sib, lon)
    sibling.start()

    def forward(s):
        src = lax.rem(a + 4 - s, 4)
        arrived(row.at[b, src], rr.at[b, src]).wait()
        loop(1, 4, lambda k: xcopy(k, src).start())

    loop(1, 4, forward)
    arrived(land.at[1 - core], sbr).wait()

    w = land[...].astype(F32)
    w = jnp.stack([w[0], w[1]], axis=1).reshape(D, 384)
    units[...] = jnp.transpose(w).astype(BF).reshape(8, HD, D)

    def each_u1(act):
        for i in range(3):
            part, h = head_unit(lon, i)
            slot = part * 4 + lax.rem(h, 4)
            g = h // 4

            @pl.when(lax.rem(h, 2) == core)
            def _():
                def dest(dyi):
                    t = dyi * 4 + lax.rem(g - b + 4, 4)
                    p, q = shifted(lat, lon, t, 1)
                    far = remote(units.at[i], u1.at[slot], u1s.at[i, dyi], u1r.at[slot], p, q)

                    @pl.when(t == 0)
                    def _():
                        if act == "start":
                            pltpu.make_async_copy(units.at[i], u1.at[slot], u1r.at[slot]).start()

                    @pl.when(t != 0)
                    def _():
                        if act == "start":
                            far.start()
                        else:
                            far.wait_send()

                loop(0, 4, dest)

    each_u1("start")

    sends = lax.rem(b, 2) == core

    def xpeer(s):
        return a * 4 + lax.rem(b + s, 4)

    def wcast(unit, dst, ssem, rsem, act):
        @pl.when(sends)
        def _():
            def along_y(d):
                p, q = shifted(lat, lon, 4 * d, 1)
                c = remote(units.at[unit], dst.at[lon], ssem.at[0, d], rsem.at[lon], p, q)
                act(c)

            def along_x(k):
                c = remote(units.at[unit], dst.at[lon], ssem.at[k, 0], rsem.at[lon], lat, xpeer(k))
                act(c)

            loop(1, 4, along_y)
            loop(1, 4, along_x)

    def wpass(dst, ssem, rsem, act, wait):
        @pl.when(sends)
        def _():
            def one(d):
                slot = lax.rem(a + d, 4) * 4 + b
                if wait:
                    arrived(dst.at[slot], rsem.at[slot]).wait()
                loop(
                    1, 4,
                    lambda k: act(remote(dst.at[slot], dst.at[slot], ssem.at[k, d], rsem.at[slot], lat, xpeer(k))),
                )

            loop(1, 4, one)

    def go(c):
        c.start()

    def left(c):
        c.wait_send()

    def wbegin(unit, dst, ssem, rsem):
        wcast(unit, dst, ssem, rsem, go)

        @pl.when(sends)
        def _():
            pltpu.make_async_copy(units.at[unit], dst.at[lon], rsem.at[lon]).start()

    def wshare(dst, rsem, fsem, k):
        slot = 2 * k + core
        return remote(dst.at[slot], dst.at[slot], fsem.at[k], rsem.at[slot], sib, lon)

    def wforward(dst, rsem, fsem):
        def one(k):
            slot = 2 * k + core

            @pl.when(jnp.logical_not((lax.rem(slot, 4) == b) & (slot // 4 != a)))
            def _():
                arrived(dst.at[slot], rsem.at[slot]).wait()

            wshare(dst, rsem, fsem, k).start()

        loop(0, 8, one)

    def wrest(dst, rsem):
        loop(0, 8, lambda k: arrived(dst.at[2 * k + 1 - core], rsem.at[2 * k + 1 - core]).wait())

    def u2slot(j, i):
        u = j * 3 + i
        part, h = u // 16, lax.rem(u, 16)
        here = h // 8 == core
        here = here if i == 0 else here & (lax.rem(place, 2) == i - 1)
        return here, part * 8 + lax.rem(h, 8)

    def u2do(act):
        for i in range(3):
            here, slot = u2slot(lon, i)

            @pl.when(here)
            def _():
                def along_y(d):
                    p, q = shifted(lat, lon, 4 * d, 1)
                    act(remote(units.at[4 + i], u2.at[slot], u2s.at[i, 0, d], u2r.at[slot], p, q))

                def along_x(k):
                    act(remote(units.at[4 + i], u2.at[slot], u2s.at[i, k, 0], u2r.at[slot], lat, xpeer(k)))

                loop(1, 4, along_y)
                loop(1, 4, along_x)
                if act is go:
                    pltpu.make_async_copy(units.at[4 + i], u2.at[slot], u2r.at[slot]).start()

    def u2on(act):
        def one(d):
            for i in range(3):
                here, slot = u2slot(lax.rem(a + d, 4) * 4 + b, i)

                @pl.when(here)
                def _():
                    if act is go:
                        arrived(u2.at[slot], u2r.at[slot]).wait()
                    loop(
                        1, 4,
                        lambda k: act(remote(u2.at[slot], u2.at[slot], u2s.at[i, k, d], u2r.at[slot], lat, xpeer(k))),
                    )

        loop(1, 4, one)

    zsib = lat + 2 - 4 * lax.rem(place, 2)

    def u2class(k):
        return lax.rem((k // 8) * 16 + core * 8 + lax.rem(k, 8), 3)

    def u2early(k):
        j = ((k // 8) * 16 + core * 8 + lax.rem(k, 8)) // 3
        here = u2class(k) != 2 - lax.rem(place, 2)
        return here & (lax.rem(j, 4) == b) & (j // 4 != a)

    def u2wait(k):
        @pl.when(jnp.logical_not(u2early(k)))
        def _():
            arrived(u2.at[k], u2r.at[k]).wait()

    def u2share(k):
        return remote(u2.at[k], u2.at[k], u2f.at[k], u2r.at[k], zsib, lon)

    def u2pass(act, lo=0, hi=24):
        def one(k):
            @pl.when(u2class(k) == 1 + lax.rem(place, 2))
            def _():
                if act == "start":
                    u2wait(k)
                    u2share(k).start()
                else:
                    u2share(k).wait_send()

        loop(lo, hi, one)

    def u2rest(k):
        @pl.when(u2class(k) != 1 + lax.rem(place, 2))
        def _():
            u2wait(k)

    def u1slot(k, c):
        return (k // 2) * 4 + lax.rem(k, 2) * 2 + c

    def u1share(k):
        slot = u1slot(k, core)
        return remote(u1.at[slot], u1.at[slot], u1f.at[k], u1r.at[slot], sib, lon)

    def u1forward(k):
        slot = u1slot(k, core)
        arrived(u1.at[slot], u1r.at[slot]).wait()
        u1share(k).start()

    u2do(go)
    loop(0, 6, u1forward)
    u2on(go)
    wbegin(3, wo1, w1s, w1r)
    loop(1, 16, lambda s: arrived(vl.at[lax.rem(lon + s, 16)], v1r.at[lax.rem(lon + s, 16)]).wait())

    def collect(s):
        src = lax.rem(b + s, 4)
        loop(0, 4, lambda aa: arrived(row.at[src, aa], rr.at[src, aa]).wait())

    loop(1, 4, collect)
    loop(0, 6, lambda k: arrived(u1.at[u1slot(k, 1 - core)], u1r.at[u1slot(k, 1 - core)]).wait())

    qkv = nt(u1[...].reshape(576, D), row[...].reshape(1024, D)).astype(BF)
    for h in range(4):
        for qb in range(4):
            q_s[qb, h] = qkv[h * HD : (h + 1) * HD, qb * 256 : (qb + 1) * 256]
        kv_s[h] = qkv[192 + h * HD : 192 + (h + 1) * HD]
        kv_s[4 + h] = qkv[384 + h * HD : 384 + (h + 1) * HD]
    ka1 = jnp.concatenate(
        [vl[(2 * (j % 2)) * 4 + j // 2] + vl[(2 * (j % 2) + 1) * 4 + j // 2] for j in range(8)], axis=1
    )
    qa1 = jnp.where(iota((16, 256), 0) == 0, 1.0, 0.0).astype(BF)
    o_s[...] = jnp.zeros_like(o_s)

    def ocopy(bb, aa):
        return remote(o_s.at[bb, aa], land_o.at[lon], os.at[bb, aa], orr.at[lon], lat, aa * 4 + bb)

    def block(qb):
        def head(h):
            k_aug = jnp.concatenate([kv_s[h], ka1], axis=0)
            q_aug = jnp.concatenate([q_s[qb, h], qa1], axis=0)
            v_aug = jnp.concatenate([kv_s[4 + h], jnp.ones((16, 1024), BF)], axis=0)
            t_s[h] = soft(k_aug, q_aug, v_aug)

        loop(0, 4, head)
        o = jnp.transpose(t_s[...].reshape(192, 256)).astype(BF)
        for aa in range(4):
            o_s[qb, aa, :, :192] = o[aa * 64 : (aa + 1) * 64]

        def send(aa):
            @pl.when(aa * 4 + qb != lon)
            def _():
                ocopy(qb, aa).start()

        loop(0, 4, send)
        u2pass("start", qb * 6, qb * 6 + 6)

        @pl.when(qb == 1)
        def _():
            wpass(wo1, w1s, w1r, go, True)


    loop(0, 4, block)
    land_o[lon] = o_s[b, a]
    wforward(wo1, w1r, w1f)
    loop(1, 16, lambda s: arrived(land_o.at[lax.rem(lon + s, 16)], orr.at[lax.rem(lon + s, 16)]).wait())
    wrest(wo1, w1r)

    heads = jnp.concatenate(
        [
            jnp.concatenate([land_o[4 * k + g][:, :192] for g in range(4)], axis=1)
            for k in range(4)
        ],
        axis=0,
    )
    middle = start_s[...] + nt(heads, wo1[...].reshape(D, D))
    start_s[...] = middle

    i = lax.broadcasted_iota(jnp.int32, (256, 256), 0)
    j = lax.broadcasted_iota(jnp.int32, (256, 256), 1)
    from_row = ((i >> 2) & 3) * 64 + (i >> 4) * 4 + (i & 3)
    perm = jnp.where(from_row == j, 1.0, 0.0).astype(BF)
    xn2 = jnp.dot(perm, normalize(middle, g2[...].reshape(1, D)), preferred_element_type=F32).astype(BF)
    x2_s[...] = xn2.reshape(16, 16, D)

    def x2copy(s):
        to = lax.rem(place + s, 16)
        return remote(
            x2_s.at[to], col.at[core, place], x2s.at[s], x2r.at[core, place], to * 2 + core, lon
        )

    def x2share(src):
        return remote(col.at[core, src], col.at[core, src], x2f.at[src], x2r.at[core, src], sib, lon)

    loop(1, 16, lambda s: x2copy(s).start())
    col[core, place] = x2_s[place]
    x2share(place).start()

    def x2forward(s):
        src = lax.rem(place + 16 - s, 16)
        arrived(col.at[core, src], x2r.at[core, src]).wait()
        x2share(src).start()

    loop(1, 16, x2forward)
    wbegin(7, wo2, w2s, w2r)

    def mwait(s):
        src = lax.rem(lat + NLAT - s, NLAT)
        c, p = lax.rem(src, 2), src // 2
        arrived(mv.at[c, p], v2r.at[c, p]).wait()

    loop(1, NLAT, mwait)
    loop(0, 24, u2rest)
    loop(0, 16, lambda k: arrived(col.at[1 - core, k], x2r.at[1 - core, k]).wait())

    qkv2[...] = nt(u2[...].reshape(1152, D), col[...].reshape(512, D)).astype(BF).reshape(24, HD, 512)
    first = jnp.where((iota((16, 128), 0) == 0) & (iota((16, 128), 1) < 4), 1.0, 0.0).astype(BF)
    fr = iota((16, 512), 0)
    same = (iota((16, 512), 1) & 3) == fr - 1
    ka2 = (nt(first, mv[...].reshape(512, 128)) + jnp.where(same, 1.0, 0.0)).astype(BF)
    other = (fr >= 1) & (fr <= 4) & jnp.logical_not(same)
    qa2 = jnp.where(fr == 0, 1.0, jnp.where(other, -1e34, 0.0)).astype(BF)

    def head2(h):
        k_aug = jnp.concatenate([qkv2[8 + h], ka2], axis=0)
        q_aug = jnp.concatenate([qkv2[h], qa2], axis=0)
        v_aug = jnp.concatenate([qkv2[16 + h], jnp.ones((16, 512), BF)], axis=0)
        t2[h] = soft(k_aug, q_aug, v_aug)

    loop(0, 8, head2)
    wpass(wo2, w2s, w2r, go, True)
    o2_s[...] = jnp.transpose(t2[...].reshape(384, 512)).astype(BF).reshape(2, 16, 16, 384)

    def bcopy(s):
        to = lax.rem(lat + s, NLAT)
        return remote(
            o2_s.at[lax.rem(to, 2), to // 2], back.at[core, place], bs.at[s], br.at[core, place], to, lon
        )

    loop(1, NLAT, lambda s: bcopy(s).start())
    back[core, place] = o2_s[core, place]
    wforward(wo2, w2r, w2f)

    def bwait(s):
        src = lax.rem(lat + NLAT - s, NLAT)
        c, p = lax.rem(src, 2), src // 2
        arrived(back.at[c, p], br.at[c, p]).wait()

    loop(1, NLAT, bwait)
    wrest(wo2, w2r)
    heads2 = jnp.concatenate([back[0].reshape(256, 384), back[1].reshape(256, 384)], axis=1)
    heads2 = lax.dot_general(
        perm, heads2, (((0,), (0,)), ((), ())), preferred_element_type=F32
    ).astype(BF)
    out[...] = (start_s[...] + nt(heads2, wo2[...].reshape(D, D))).astype(BF).reshape(4, 64, D)

    loop(1, 16, lambda s: wcopy(s).wait_send())
    sibling.wait_send()
    loop(1, 16, lambda s: v1copy(s).wait_send())
    loop(1, NLAT, lambda s: v2copy(s).wait_send())
    loop(1, 4, lambda s: ycopy(s).wait_send())
    loop(1, 4, lambda s: loop(0, 4, lambda aa: xcopy(s, aa).wait_send()))
    each_u1("finish")
    loop(0, 6, lambda k: u1share(k).wait_send())

    wcast(3, wo1, w1s, w1r, left)
    wpass(wo1, w1s, w1r, left, False)
    wcast(7, wo2, w2s, w2r, left)
    wpass(wo2, w2s, w2r, left, False)

    loop(0, 8, lambda k: wshare(wo1, w1r, w1f, k).wait_send())
    loop(0, 8, lambda k: wshare(wo2, w2r, w2f, k).wait_send())
    u2do(left)
    u2on(left)
    u2pass("finish")

    def osent(k):
        bb, aa = lax.rem(k, 4), k // 4

        @pl.when(k != lon)
        def _():
            ocopy(bb, aa).wait_send()

    loop(0, 16, osent)
    loop(1, 16, lambda s: x2copy(s).wait_send())
    loop(0, 16, lambda k: x2share(k).wait_send())
    loop(1, NLAT, lambda s: bcopy(s).wait_send())


def pair(*args):
    return pl.pallas_call(
        pair_kernel,
        out_shape=jax.ShapeDtypeStruct((4, 64, D), BF),
        in_specs=[VMEM] * len(args),
        out_specs=VMEM,
        scratch_shapes=[
            pltpu.VMEM((24, 384), BF),
            pltpu.VMEM((8, D), F32),
            pltpu.VMEM((4, 16, 128), BF),
            pltpu.VMEM((16, 16, 128), BF),
            pltpu.VMEM((2, 16, 24, 384), BF),
            pltpu.VMEM((8, HD, D), BF),
            pltpu.VMEM((256, D), F32),
            pltpu.VMEM((4, 64, D), BF),
            pltpu.VMEM((4, 4, 64, D), BF),
            pltpu.VMEM((12, HD, D), BF),
            pltpu.VMEM((16, HD, D), BF),
            pltpu.VMEM((24, HD, D), BF),
            pltpu.VMEM((16, HD, D), BF),
            pltpu.VMEM((16, 16, 128), BF),
            pltpu.VMEM((2, 16, 16, 128), BF),
            pltpu.VMEM((4, 4, HD, 256), BF),
            pltpu.VMEM((8, HD, 1024), BF),
            pltpu.VMEM((4, HD, 256), F32),
            pltpu.VMEM((4, 4, 64, 256), BF),
            pltpu.VMEM((16, 64, 256), BF),
            pltpu.VMEM((16, 16, D), BF),
            pltpu.VMEM((2, 16, 16, D), BF),
            pltpu.VMEM((24, HD, 512), BF),
            pltpu.VMEM((8, HD, 512), F32),
            pltpu.VMEM((2, 16, 16, 384), BF),
            pltpu.VMEM((2, 16, 16, 384), BF),
            DMA((16,)), DMA((16,)), DMA, DMA, DMA((16,)), DMA((16,)), DMA((NLAT,)), DMA((2, 16)),
            DMA((4,)), DMA((4, 4)), DMA((4, 4)), DMA((3, 4)), DMA((12,)), DMA((6,)),
            DMA((4, 4)), DMA((16,)), DMA((8,)), DMA((3, 4, 4)), DMA((24,)), DMA((24,)),
            DMA((4, 4)), DMA((16,)), DMA((8,)), DMA((4, 4)), DMA((16,)),
            DMA((16,)), DMA((2, 16)), DMA((16,)), DMA((NLAT,)), DMA((2, 16)),
        ],
        compiler_params=pltpu.CompilerParams(
            collective_id=0, has_side_effects=True, vmem_limit_bytes=LIMIT
        ),
    )(*args)


def local(
    tokens, source_id, valid, source_table, gain_lon, gain_lat, wqkv_lon, wout_lon, wqkv_lat, wout_lat
):
    return pair(
        tokens, source_id, valid, source_table, gain_lon, gain_lat, wqkv_lon, wout_lon, wqkv_lat, wout_lat
    )


def solution(mesh):
    placed = (
        P("lat", "lon", None),
        P("lat", "lon"),
        P("lat", "lon"),
        P(),
        P(),
        P(),
        P("lat", "lon"),
        P("lat", "lon"),
        P("lat", "lon"),
        P("lat", "lon"),
    )
    return jax.shard_map(
        local, mesh=mesh, in_specs=placed, out_specs=P("lat", "lon", None), check_vma=False
    )
```

```python
import functools

import jax
import jax.numpy as jnp
from jax import lax
from jax.experimental import pallas as pl
from jax.experimental.pallas import tpu as pltpu
from jax.sharding import PartitionSpec as P

HEADS = 16
HD = 48
D = 768
NLAT = 32
NLON = 16
MESH = pl.DeviceIdType.MESH
BF = jnp.bfloat16
F32 = jnp.float32
VMEM = pl.BlockSpec(memory_space=pltpu.VMEM)
DMA = pltpu.SemaphoreType.DMA
SCALE2 = float(1.4426950408889634 / (48.0**0.5))
LIMIT = 56 * 1024 * 1024


def normalize(x, gain):
    scale = lax.rsqrt(jnp.mean(x * x, axis=-1, keepdims=True) + 1e-06)
    return (x * scale * gain).astype(BF)


def nt(x, y):
    return lax.dot_general(x, y, (((1,), (1,)), ((), ())), preferred_element_type=F32)


def where_am_i():
    return lax.axis_index("lat"), lax.axis_index("lon")


def remote(src, dst, send, recv, lat, lon):
    return pltpu.make_async_remote_copy(
        src_ref=src,
        dst_ref=dst,
        send_sem=send,
        recv_sem=recv,
        device_id=(lat, lon),
        device_id_type=MESH,
    )


def shifted(lat, lon, t, sign):
    core = lax.rem(lat, 2)
    dyi = t // 4
    off = dyi + 4 * (dyi // 3) + 4 * core * ((dyi // 2) * (3 - dyi))
    y = (lat // 16) * 4 + lon // 4
    y2 = lax.rem(y + off, 8) if sign > 0 else lax.rem(y + 8 - off, 8)
    dx = lax.rem(t, 4)
    x = lax.rem(lon, 4)
    x2 = lax.rem(x + dx, 4) if sign > 0 else lax.rem(x + 4 - dx, 4)
    return lax.rem(lat, 16) + 16 * (y2 // 4), lax.rem(y2, 4) * 4 + x2


def signal(sem, lat, lon):
    pl.semaphore_signal(sem, inc=1, device_id=(lat, lon), device_id_type=MESH)


def loop(lo, hi, body):
    def step(i, carry):
        body(i)
        return carry

    lax.fori_loop(lo, hi, step, 0)


def head_unit(lon, i):
    u = lon * 3 + i
    return u // 16, lax.rem(u, 16)


def soft(k_aug, q_aug, v_aug):
    s = lax.dot_general(k_aug, q_aug, (((0,), (0,)), ((), ())), preferred_element_type=F32)
    m = jnp.max(s, axis=0, keepdims=True)
    p = jnp.exp2((s - m) * SCALE2).astype(BF)
    o = jnp.dot(v_aug, p, preferred_element_type=F32)
    return o[:HD] / o[HD : HD + 1]


def iota(shape, axis):
    return lax.broadcasted_iota(jnp.int32, shape, axis)


def arrived(ref, sem):
    return pltpu.make_async_copy(ref, ref, sem)


def pair_kernel(
    tok, sid, valid, table, g1, g2, wq1, wp1, wq2, wp2, out,
    shard, table_s, v1, v2,
    land, units, start_s, xn_s, row, u1, wo1, u2, wo2, vl, mv, q_s, kv_s, t_s, o_s, land_o,
    x2_s, col, qkv2, t2, o2_s, back,
    s1s, s1r, sbs, sbr, v1s, v1r, v2s, v2r, ys, xs, rr, u1s, u1r, u1f, w1s, w1r, w1f, u2s, u2r,
    u2f, w2s, w2r, w2f, os, orr, x2s, x2r, x2f, bs, br,
):
    lat, lon = where_am_i()
    a, b = lon // 4, lax.rem(lon, 4)
    core, place = lax.rem(lat, 2), lat // 2
    sib = lat + 1 - 2 * core

    bar = pltpu.get_barrier_semaphore()
    loop(1, NLAT, lambda s: signal(bar, lax.rem(lat + s, NLAT), lon))

    def greet(t):
        p, q = shifted(lat, lon, t, -1)
        signal(bar, p, q)
        signal(bar, lat, lax.rem(lon + t, NLON))

    loop(1, 16, greet)

    shard[...] = jnp.concatenate(
        [w[...].astype(F32) for w in (wq1, wp1, wq2, wp2)], axis=1
    ).astype(BF)
    land[core, place] = shard[...]
    pl.semaphore_wait(bar, 61)

    def wcopy(s):
        to = lax.rem(place + s, 16)
        return remote(shard, land.at[core, place], s1s.at[s], s1r.at[place], to * 2 + core, lon)

    loop(1, 16, lambda s: wcopy(s).start())

    def ycopy(s):
        to = lax.rem(a + s, 4)
        return remote(xn_s.at[to], row.at[b, a], ys.at[s], rr.at[b, a], lat, to * 4 + b)

    def xcopy(s, aa):
        to = lax.rem(b + s, 4)
        return remote(row.at[b, aa], row.at[b, aa], xs.at[s, aa], rr.at[b, aa], lat, a * 4 + to)

    table_s[...] = jnp.zeros_like(table_s)
    table_s[0:5] = table[...]
    ids = sid[...]
    for k in range(4):
        onehot = jnp.where(iota((8, 64), 0) == ids[k : k + 1], 1.0, 0.0)
        emb = lax.dot_general(
            onehot, table_s[...], (((0,), (0,)), ((), ())),
            precision=lax.Precision.HIGHEST, preferred_element_type=F32,
        )
        first = tok[k].astype(F32) + emb
        start_s[k * 64 : (k + 1) * 64] = first
        xn_s[k] = normalize(first, g1[...].reshape(1, D))

    loop(1, 4, lambda s: ycopy(s).start())
    row[b, a] = xn_s[a]
    loop(1, 4, lambda s: xcopy(s, a).start())

    bias = jnp.where(valid[...] > 0, 0.0, -1e30)
    for k in range(4):
        line = jnp.where(iota((16, 64), 0) == 0, bias[k : k + 1], 0.0)
        none = jnp.zeros((16, 64), F32)
        v1[k] = jnp.where(
            lax.rem(a, 2) == 0,
            jnp.concatenate([line, none], axis=1),
            jnp.concatenate([none, line], axis=1),
        ).astype(BF)
    token, lane = iota((256, 64), 0), iota((256, 64), 1)
    picks = jnp.where((token >> 4) * 4 + (token & 3) == lane, 1.0, 0.0).astype(BF)
    tall = jnp.concatenate([bias, jnp.zeros((124, 64), F32)], axis=0).astype(BF)
    v2all = nt(picks, tall)
    v2all = jnp.where(iota((256, 128), 1) == ((iota((256, 128), 0) >> 2) & 3), v2all, 0.0)
    v2[...] = v2all.astype(BF).reshape(16, 16, 128)

    def v1copy(s):
        to = lax.rem(lon + s, NLON)
        return remote(v1.at[to // 4], vl.at[lon], v1s.at[s], v1r.at[lon], lat, to)

    def v2copy(s):
        to = lax.rem(place + s, 16)
        return remote(
            v2.at[to], mv.at[core, place], v2s.at[s], v2r.at[core, place], to * 2 + core, lon
        )

    loop(1, 16, lambda s: v1copy(s).start())
    vl[lon] = v1[a]
    mv[core, place] = v2[place]

    def missing(s):
        src = lax.rem(place + 16 - s, 16)
        arrived(land.at[core, src], s1r.at[src]).wait()

    loop(1, 16, missing)
    sibling = remote(land.at[core], land.at[core], sbs, sbr, sib, lon)
    sibling.start()

    def forward(s):
        src = lax.rem(a + 4 - s, 4)
        arrived(row.at[b, src], rr.at[b, src]).wait()
        loop(1, 4, lambda k: xcopy(k, src).start())

    loop(1, 4, forward)
    arrived(land.at[1 - core], sbr).wait()

    w = land[...].astype(F32)
    w = jnp.stack([w[0], w[1]], axis=1).reshape(D, 384)
    units[...] = jnp.transpose(w).astype(BF).reshape(8, HD, D)

    def each_u1(act):
        for i in range(3):
            part, h = head_unit(lon, i)
            slot = part * 4 + lax.rem(h, 4)
            g = h // 4

            @pl.when(lax.rem(h, 2) == core)
            def _():
                def dest(dyi):
                    t = dyi * 4 + lax.rem(g - b + 4, 4)
                    p, q = shifted(lat, lon, t, 1)
                    far = remote(units.at[i], u1.at[slot], u1s.at[i, dyi], u1r.at[slot], p, q)

                    @pl.when(t == 0)
                    def _():
                        if act == "start":
                            pltpu.make_async_copy(units.at[i], u1.at[slot], u1r.at[slot]).start()

                    @pl.when(t != 0)
                    def _():
                        if act == "start":
                            far.start()
                        else:
                            far.wait_send()

                loop(0, 4, dest)

    each_u1("start")

    sends = lax.rem(b, 2) == core

    def xpeer(s):
        return a * 4 + lax.rem(b + s, 4)

    def wcast(unit, dst, ssem, rsem, act):
        @pl.when(sends)
        def _():
            def along_y(d):
                p, q = shifted(lat, lon, 4 * d, 1)
                c = remote(units.at[unit], dst.at[lon], ssem.at[0, d], rsem.at[lon], p, q)
                act(c)

            def along_x(k):
                c = remote(units.at[unit], dst.at[lon], ssem.at[k, 0], rsem.at[lon], lat, xpeer(k))
                act(c)

            loop(1, 4, along_y)
            loop(1, 4, along_x)

    def wpass(dst, ssem, rsem, act, wait):
        @pl.when(sends)
        def _():
            def one(d):
                slot = lax.rem(a + d, 4) * 4 + b
                if wait:
                    arrived(dst.at[slot], rsem.at[slot]).wait()
                loop(
                    1, 4,
                    lambda k: act(remote(dst.at[slot], dst.at[slot], ssem.at[k, d], rsem.at[slot], lat, xpeer(k))),
                )

            loop(1, 4, one)

    def go(c):
        c.start()

    def left(c):
        c.wait_send()

    def wbegin(unit, dst, ssem, rsem):
        wcast(unit, dst, ssem, rsem, go)

        @pl.when(sends)
        def _():
            pltpu.make_async_copy(units.at[unit], dst.at[lon], rsem.at[lon]).start()

    def wshare(dst, rsem, fsem, k):
        slot = 2 * k + core
        return remote(dst.at[slot], dst.at[slot], fsem.at[k], rsem.at[slot], sib, lon)

    def wforward(dst, rsem, fsem):
        def one(k):
            slot = 2 * k + core

            @pl.when(jnp.logical_not((lax.rem(slot, 4) == b) & (slot // 4 != a)))
            def _():
                arrived(dst.at[slot], rsem.at[slot]).wait()

            wshare(dst, rsem, fsem, k).start()

        loop(0, 8, one)

    def wrest(dst, rsem):
        loop(0, 8, lambda k: arrived(dst.at[2 * k + 1 - core], rsem.at[2 * k + 1 - core]).wait())

    def u2slot(j, i):
        u = j * 3 + i
        part, h = u // 16, lax.rem(u, 16)
        here = h // 8 == core
        here = here if i == 0 else here & (lax.rem(place, 2) == i - 1)
        return here, part * 8 + lax.rem(h, 8)

    def u2do(act):
        for i in range(3):
            here, slot = u2slot(lon, i)

            @pl.when(here)
            def _():
                def along_y(d):
                    p, q = shifted(lat, lon, 4 * d, 1)
                    act(remote(units.at[4 + i], u2.at[slot], u2s.at[i, 0, d], u2r.at[slot], p, q))

                def along_x(k):
                    act(remote(units.at[4 + i], u2.at[slot], u2s.at[i, k, 0], u2r.at[slot], lat, xpeer(k)))

                loop(1, 4, along_y)
                loop(1, 4, along_x)
                if act is go:
                    pltpu.make_async_copy(units.at[4 + i], u2.at[slot], u2r.at[slot]).start()

    def u2on(act):
        def one(d):
            for i in range(3):
                here, slot = u2slot(lax.rem(a + d, 4) * 4 + b, i)

                @pl.when(here)
                def _():
                    if act is go:
                        arrived(u2.at[slot], u2r.at[slot]).wait()
                    loop(
                        1, 4,
                        lambda k: act(remote(u2.at[slot], u2.at[slot], u2s.at[i, k, d], u2r.at[slot], lat, xpeer(k))),
                    )

        loop(1, 4, one)

    zsib = lat + 2 - 4 * lax.rem(place, 2)

    def u2class(k):
        return lax.rem((k // 8) * 16 + core * 8 + lax.rem(k, 8), 3)

    def u2early(k):
        j = ((k // 8) * 16 + core * 8 + lax.rem(k, 8)) // 3
        here = u2class(k) != 2 - lax.rem(place, 2)
        return here & (lax.rem(j, 4) == b) & (j // 4 != a)

    def u2wait(k):
        @pl.when(jnp.logical_not(u2early(k)))
        def _():
            arrived(u2.at[k], u2r.at[k]).wait()

    def u2share(k):
        return remote(u2.at[k], u2.at[k], u2f.at[k], u2r.at[k], zsib, lon)

    def u2pass(act, lo=0, hi=24):
        def one(k):
            @pl.when(u2class(k) == 1 + lax.rem(place, 2))
            def _():
                if act == "start":
                    u2wait(k)
                    u2share(k).start()
                else:
                    u2share(k).wait_send()

        loop(lo, hi, one)

    def u2rest(k):
        @pl.when(u2class(k) != 1 + lax.rem(place, 2))
        def _():
            u2wait(k)

    def u1slot(k, c):
        return (k // 2) * 4 + lax.rem(k, 2) * 2 + c

    def u1share(k):
        slot = u1slot(k, core)
        return remote(u1.at[slot], u1.at[slot], u1f.at[k], u1r.at[slot], sib, lon)

    def u1forward(k):
        slot = u1slot(k, core)
        arrived(u1.at[slot], u1r.at[slot]).wait()
        u1share(k).start()

    u2do(go)
    loop(1, 16, lambda s: v2copy(s).start())
    loop(0, 6, u1forward)
    u2on(go)
    wbegin(3, wo1, w1s, w1r)
    loop(1, 16, lambda s: arrived(vl.at[lax.rem(lon + s, 16)], v1r.at[lax.rem(lon + s, 16)]).wait())

    def collect(s):
        src = lax.rem(b + s, 4)
        loop(0, 4, lambda aa: arrived(row.at[src, aa], rr.at[src, aa]).wait())

    loop(1, 4, collect)
    loop(0, 6, lambda k: arrived(u1.at[u1slot(k, 1 - core)], u1r.at[u1slot(k, 1 - core)]).wait())

    qkv = nt(u1[...].reshape(576, D), row[...].reshape(1024, D)).astype(BF)
    for h in range(4):
        for qb in range(4):
            q_s[qb, h] = qkv[h * HD : (h + 1) * HD, qb * 256 : (qb + 1) * 256]
        kv_s[h] = qkv[192 + h * HD : 192 + (h + 1) * HD]
        kv_s[4 + h] = qkv[384 + h * HD : 384 + (h + 1) * HD]
    ka1 = jnp.concatenate(
        [vl[(2 * (j % 2)) * 4 + j // 2] + vl[(2 * (j % 2) + 1) * 4 + j // 2] for j in range(8)], axis=1
    )
    qa1 = jnp.where(iota((16, 256), 0) == 0, 1.0, 0.0).astype(BF)
    o_s[...] = jnp.zeros_like(o_s)

    def ocopy(bb, aa):
        return remote(o_s.at[bb, aa], land_o.at[lon], os.at[bb, aa], orr.at[lon], lat, aa * 4 + bb)

    def block(step):
        qb = lax.rem(b + 1 + step, 4)

        def head(h):
            k_aug = jnp.concatenate([kv_s[h], ka1], axis=0)
            q_aug = jnp.concatenate([q_s[qb, h], qa1], axis=0)
            v_aug = jnp.concatenate([kv_s[4 + h], jnp.ones((16, 1024), BF)], axis=0)
            t_s[h] = soft(k_aug, q_aug, v_aug)

        loop(0, 4, head)
        o = jnp.transpose(t_s[...].reshape(192, 256)).astype(BF)
        for aa in range(4):
            o_s[qb, aa, :, :192] = o[aa * 64 : (aa + 1) * 64]

        def send(k):
            aa = lax.rem(a + 1 + k, 4)

            @pl.when(aa * 4 + qb != lon)
            def _():
                ocopy(qb, aa).start()

        loop(0, 4, send)
        u2pass("start", step * 6, step * 6 + 6)

        @pl.when(step == 1)
        def _():
            wpass(wo1, w1s, w1r, go, True)


    loop(0, 4, block)

    def mwait(s):
        src = lax.rem(place + 16 - s, 16)
        arrived(mv.at[core, src], v2r.at[core, src]).wait()

    loop(1, 16, mwait)
    mshare = remote(mv.at[core], mv.at[core], v2s.at[0], v2r.at[core, 0], sib, lon)
    mshare.start()
    land_o[lon] = o_s[b, a]
    wforward(wo1, w1r, w1f)
    loop(1, 16, lambda s: arrived(land_o.at[lax.rem(lon + s, 16)], orr.at[lax.rem(lon + s, 16)]).wait())
    wrest(wo1, w1r)

    heads = jnp.concatenate(
        [
            jnp.concatenate([land_o[4 * k + g][:, :192] for g in range(4)], axis=1)
            for k in range(4)
        ],
        axis=0,
    )
    middle = start_s[...] + nt(heads, wo1[...].reshape(D, D))
    start_s[...] = middle

    i = lax.broadcasted_iota(jnp.int32, (256, 256), 0)
    j = lax.broadcasted_iota(jnp.int32, (256, 256), 1)
    from_row = ((i >> 2) & 3) * 64 + (i >> 4) * 4 + (i & 3)
    perm = jnp.where(from_row == j, 1.0, 0.0).astype(BF)
    xn2 = jnp.dot(perm, normalize(middle, g2[...].reshape(1, D)), preferred_element_type=F32).astype(BF)
    x2_s[...] = xn2.reshape(16, 16, D)

    def x2copy(s):
        to = lax.rem(place + s, 16)
        return remote(
            x2_s.at[to], col.at[core, place], x2s.at[s], x2r.at[core, place], to * 2 + core, lon
        )

    def x2share(src):
        return remote(col.at[core, src], col.at[core, src], x2f.at[src], x2r.at[core, src], sib, lon)

    loop(1, 16, lambda s: x2copy(s).start())
    col[core, place] = x2_s[place]
    x2share(place).start()

    def x2forward(s):
        src = lax.rem(place + 16 - s, 16)
        arrived(col.at[core, src], x2r.at[core, src]).wait()
        x2share(src).start()

    loop(1, 16, x2forward)
    wbegin(7, wo2, w2s, w2r)

    arrived(mv.at[1 - core], v2r.at[1 - core, 0]).wait()
    loop(0, 24, u2rest)
    loop(0, 16, lambda k: arrived(col.at[1 - core, k], x2r.at[1 - core, k]).wait())

    qkv2[...] = nt(u2[...].reshape(1152, D), col[...].reshape(512, D)).astype(BF).reshape(24, HD, 512)
    first = jnp.where((iota((16, 128), 0) == 0) & (iota((16, 128), 1) < 4), 1.0, 0.0).astype(BF)
    fr = iota((16, 512), 0)
    same = (iota((16, 512), 1) & 3) == fr - 1
    ka2 = (nt(first, mv[...].reshape(512, 128)) + jnp.where(same, 1.0, 0.0)).astype(BF)
    other = (fr >= 1) & (fr <= 4) & jnp.logical_not(same)
    qa2 = jnp.where(fr == 0, 1.0, jnp.where(other, -1e34, 0.0)).astype(BF)

    def head2(h):
        k_aug = jnp.concatenate([qkv2[8 + h], ka2], axis=0)
        q_aug = jnp.concatenate([qkv2[h], qa2], axis=0)
        v_aug = jnp.concatenate([qkv2[16 + h], jnp.ones((16, 512), BF)], axis=0)
        t2[h] = soft(k_aug, q_aug, v_aug)

    loop(0, 8, head2)
    wpass(wo2, w2s, w2r, go, True)
    o2_s[...] = jnp.transpose(t2[...].reshape(384, 512)).astype(BF).reshape(2, 16, 16, 384)

    def bcopy(s):
        to = lax.rem(lat + s, NLAT)
        return remote(
            o2_s.at[lax.rem(to, 2), to // 2], back.at[core, place], bs.at[s], br.at[core, place], to, lon
        )

    loop(1, NLAT, lambda s: bcopy(s).start())
    back[core, place] = o2_s[core, place]
    wforward(wo2, w2r, w2f)

    def bwait(s):
        src = lax.rem(lat + NLAT - s, NLAT)
        c, p = lax.rem(src, 2), src // 2
        arrived(back.at[c, p], br.at[c, p]).wait()

    loop(1, NLAT, bwait)
    wrest(wo2, w2r)
    heads2 = jnp.concatenate([back[0].reshape(256, 384), back[1].reshape(256, 384)], axis=1)
    heads2 = lax.dot_general(
        perm, heads2, (((0,), (0,)), ((), ())), preferred_element_type=F32
    ).astype(BF)
    out[...] = (start_s[...] + nt(heads2, wo2[...].reshape(D, D))).astype(BF).reshape(4, 64, D)

    loop(1, 16, lambda s: wcopy(s).wait_send())
    sibling.wait_send()
    loop(1, 16, lambda s: v1copy(s).wait_send())
    loop(1, 16, lambda s: v2copy(s).wait_send())
    mshare.wait_send()
    loop(1, 4, lambda s: ycopy(s).wait_send())
    loop(1, 4, lambda s: loop(0, 4, lambda aa: xcopy(s, aa).wait_send()))
    each_u1("finish")
    loop(0, 6, lambda k: u1share(k).wait_send())

    wcast(3, wo1, w1s, w1r, left)
    wpass(wo1, w1s, w1r, left, False)
    wcast(7, wo2, w2s, w2r, left)
    wpass(wo2, w2s, w2r, left, False)

    loop(0, 8, lambda k: wshare(wo1, w1r, w1f, k).wait_send())
    loop(0, 8, lambda k: wshare(wo2, w2r, w2f, k).wait_send())
    u2do(left)
    u2on(left)
    u2pass("finish")

    def osent(k):
        bb, aa = lax.rem(k, 4), k // 4

        @pl.when(k != lon)
        def _():
            ocopy(bb, aa).wait_send()

    loop(0, 16, osent)
    loop(1, 16, lambda s: x2copy(s).wait_send())
    loop(0, 16, lambda k: x2share(k).wait_send())
    loop(1, NLAT, lambda s: bcopy(s).wait_send())


def pair(*args):
    return pl.pallas_call(
        pair_kernel,
        out_shape=jax.ShapeDtypeStruct((4, 64, D), BF),
        in_specs=[VMEM] * len(args),
        out_specs=VMEM,
        scratch_shapes=[
            pltpu.VMEM((24, 384), BF),
            pltpu.VMEM((8, D), F32),
            pltpu.VMEM((4, 16, 128), BF),
            pltpu.VMEM((16, 16, 128), BF),
            pltpu.VMEM((2, 16, 24, 384), BF),
            pltpu.VMEM((8, HD, D), BF),
            pltpu.VMEM((256, D), F32),
            pltpu.VMEM((4, 64, D), BF),
            pltpu.VMEM((4, 4, 64, D), BF),
            pltpu.VMEM((12, HD, D), BF),
            pltpu.VMEM((16, HD, D), BF),
            pltpu.VMEM((24, HD, D), BF),
            pltpu.VMEM((16, HD, D), BF),
            pltpu.VMEM((16, 16, 128), BF),
            pltpu.VMEM((2, 16, 16, 128), BF),
            pltpu.VMEM((4, 4, HD, 256), BF),
            pltpu.VMEM((8, HD, 1024), BF),
            pltpu.VMEM((4, HD, 256), F32),
            pltpu.VMEM((4, 4, 64, 256), BF),
            pltpu.VMEM((16, 64, 256), BF),
            pltpu.VMEM((16, 16, D), BF),
            pltpu.VMEM((2, 16, 16, D), BF),
            pltpu.VMEM((24, HD, 512), BF),
            pltpu.VMEM((8, HD, 512), F32),
            pltpu.VMEM((2, 16, 16, 384), BF),
            pltpu.VMEM((2, 16, 16, 384), BF),
            DMA((16,)), DMA((16,)), DMA, DMA, DMA((16,)), DMA((16,)), DMA((NLAT,)), DMA((2, 16)),
            DMA((4,)), DMA((4, 4)), DMA((4, 4)), DMA((3, 4)), DMA((12,)), DMA((6,)),
            DMA((4, 4)), DMA((16,)), DMA((8,)), DMA((3, 4, 4)), DMA((24,)), DMA((24,)),
            DMA((4, 4)), DMA((16,)), DMA((8,)), DMA((4, 4)), DMA((16,)),
            DMA((16,)), DMA((2, 16)), DMA((16,)), DMA((NLAT,)), DMA((2, 16)),
        ],
        compiler_params=pltpu.CompilerParams(
            collective_id=0, has_side_effects=True, vmem_limit_bytes=LIMIT
        ),
    )(*args)


def local(
    tokens, source_id, valid, source_table, gain_lon, gain_lat, wqkv_lon, wout_lon, wqkv_lat, wout_lat
):
    return pair(
        tokens, source_id, valid, source_table, gain_lon, gain_lat, wqkv_lon, wout_lon, wqkv_lat, wout_lat
    )


def solution(mesh):
    placed = (
        P("lat", "lon", None),
        P("lat", "lon"),
        P("lat", "lon"),
        P(),
        P(),
        P(),
        P("lat", "lon"),
        P("lat", "lon"),
        P("lat", "lon"),
        P("lat", "lon"),
    )
    return jax.shard_map(
        local, mesh=mesh, in_specs=placed, out_specs=P("lat", "lon", None), check_vma=False
    )
```

```python
import functools

import jax
import jax.numpy as jnp
from jax import lax
from jax.experimental import pallas as pl
from jax.experimental.pallas import tpu as pltpu
from jax.sharding import PartitionSpec as P

HEADS = 16
HD = 48
D = 768
NLAT = 32
NLON = 16
MESH = pl.DeviceIdType.MESH
BF = jnp.bfloat16
F32 = jnp.float32
VMEM = pl.BlockSpec(memory_space=pltpu.VMEM)
DMA = pltpu.SemaphoreType.DMA
SCALE2 = float(1.4426950408889634 / (48.0**0.5))
LIMIT = 56 * 1024 * 1024


def normalize(x, gain):
    scale = lax.rsqrt(jnp.mean(x * x, axis=-1, keepdims=True) + 1e-06)
    return (x * scale * gain).astype(BF)


def nt(x, y):
    return lax.dot_general(x, y, (((1,), (1,)), ((), ())), preferred_element_type=F32)


def where_am_i():
    return lax.axis_index("lat"), lax.axis_index("lon")


def remote(src, dst, send, recv, lat, lon):
    return pltpu.make_async_remote_copy(
        src_ref=src,
        dst_ref=dst,
        send_sem=send,
        recv_sem=recv,
        device_id=(lat, lon),
        device_id_type=MESH,
    )


def shifted(lat, lon, t, sign):
    core = lax.rem(lat, 2)
    dyi = t // 4
    off = dyi + 4 * (dyi // 3) + 4 * core * ((dyi // 2) * (3 - dyi))
    y = (lat // 16) * 4 + lon // 4
    y2 = lax.rem(y + off, 8) if sign > 0 else lax.rem(y + 8 - off, 8)
    dx = lax.rem(t, 4)
    x = lax.rem(lon, 4)
    x2 = lax.rem(x + dx, 4) if sign > 0 else lax.rem(x + 4 - dx, 4)
    return lax.rem(lat, 16) + 16 * (y2 // 4), lax.rem(y2, 4) * 4 + x2


def signal(sem, lat, lon):
    pl.semaphore_signal(sem, inc=1, device_id=(lat, lon), device_id_type=MESH)


def loop(lo, hi, body):
    def step(i, carry):
        body(i)
        return carry

    lax.fori_loop(lo, hi, step, 0)


def head_unit(lon, i):
    u = lon * 3 + i
    return u // 16, lax.rem(u, 16)


def soft(k_aug, q_aug, v_aug):
    s = lax.dot_general(k_aug, q_aug, (((0,), (0,)), ((), ())), preferred_element_type=F32)
    m = jnp.max(s, axis=0, keepdims=True)
    p = jnp.exp2((s - m) * SCALE2).astype(BF)
    o = jnp.dot(v_aug, p, preferred_element_type=F32)
    return o[:HD] / o[HD : HD + 1]


def iota(shape, axis):
    return lax.broadcasted_iota(jnp.int32, shape, axis)


def arrived(ref, sem):
    return pltpu.make_async_copy(ref, ref, sem)


def pair_kernel(
    tok, sid, valid, table, g1, g2, wq1, wp1, wq2, wp2, out,
    shard, table_s, v1, v2,
    land, units, start_s, xn_s, row, u1, wo1, u2, wo2, vl, mv, q_s, kv_s, t_s, o_s, land_o,
    x2_s, col, qkv2, t2, o2_s, back,
    s1s, s1r, sbs, sbr, v1s, v1r, v2s, v2r, ys, xs, rr, u1s, u1r, u1f, w1s, w1r, w1f, u2s, u2r,
    u2f, w2s, w2r, w2f, os, orr, x2s, x2r, x2f, bs, br,
):
    lat, lon = where_am_i()
    a, b = lon // 4, lax.rem(lon, 4)
    core, place = lax.rem(lat, 2), lat // 2
    sib = lat + 1 - 2 * core

    bar = pltpu.get_barrier_semaphore()
    loop(1, NLAT, lambda s: signal(bar, lax.rem(lat + s, NLAT), lon))

    def greet(t):
        p, q = shifted(lat, lon, t, -1)
        signal(bar, p, q)
        signal(bar, lat, lax.rem(lon + t, NLON))

    loop(1, 16, greet)

    shard[...] = jnp.concatenate(
        [w[...].astype(F32) for w in (wq1, wp1, wq2, wp2)], axis=1
    ).astype(BF)
    land[core, place] = shard[...]
    pl.semaphore_wait(bar, 61)

    def wcopy(s):
        to = lax.rem(place + s, 16)
        return remote(shard, land.at[core, place], s1s.at[s], s1r.at[place], to * 2 + core, lon)

    loop(1, 16, lambda s: wcopy(s).start())

    def ycopy(s):
        to = lax.rem(a + s, 4)
        return remote(xn_s.at[to], row.at[b, a], ys.at[s], rr.at[b, a], lat, to * 4 + b)

    def xcopy(s, aa):
        to = lax.rem(b + s, 4)
        return remote(row.at[b, aa], row.at[b, aa], xs.at[s, aa], rr.at[b, aa], lat, a * 4 + to)

    table_s[...] = jnp.zeros_like(table_s)
    table_s[0:5] = table[...]
    ids = sid[...]
    for k in range(4):
        onehot = jnp.where(iota((8, 64), 0) == ids[k : k + 1], 1.0, 0.0)
        emb = lax.dot_general(
            onehot, table_s[...], (((0,), (0,)), ((), ())),
            precision=lax.Precision.HIGHEST, preferred_element_type=F32,
        )
        first = tok[k].astype(F32) + emb
        start_s[k * 64 : (k + 1) * 64] = first
        xn_s[k] = normalize(first, g1[...].reshape(1, D))

    loop(1, 4, lambda s: ycopy(s).start())
    row[b, a] = xn_s[a]
    loop(1, 4, lambda s: xcopy(s, a).start())

    bias = jnp.where(valid[...] > 0, 0.0, -1e30)
    for k in range(4):
        line = jnp.where(iota((16, 64), 0) == 0, bias[k : k + 1], 0.0)
        none = jnp.zeros((16, 64), F32)
        v1[k] = jnp.where(
            lax.rem(a, 2) == 0,
            jnp.concatenate([line, none], axis=1),
            jnp.concatenate([none, line], axis=1),
        ).astype(BF)
    token, lane = iota((256, 64), 0), iota((256, 64), 1)
    picks = jnp.where((token >> 4) * 4 + (token & 3) == lane, 1.0, 0.0).astype(BF)
    tall = jnp.concatenate([bias, jnp.zeros((124, 64), F32)], axis=0).astype(BF)
    v2all = nt(picks, tall)
    v2all = jnp.where(iota((256, 128), 1) == ((iota((256, 128), 0) >> 2) & 3), v2all, 0.0)
    v2[...] = v2all.astype(BF).reshape(16, 16, 128)

    def v1copy(s):
        to = lax.rem(lon + s, NLON)
        return remote(v1.at[to // 4], vl.at[lon], v1s.at[s], v1r.at[lon], lat, to)

    def v2copy(s):
        to = lax.rem(place + s, 16)
        return remote(
            v2.at[to], mv.at[core, place], v2s.at[s], v2r.at[core, place], to * 2 + core, lon
        )

    vl[lon] = v1[a]
    mv[core, place] = v2[place]

    def missing(s):
        src = lax.rem(place + 16 - s, 16)
        arrived(land.at[core, src], s1r.at[src]).wait()

    loop(1, 16, missing)
    sibling = remote(land.at[core], land.at[core], sbs, sbr, sib, lon)
    sibling.start()

    def forward(s):
        src = lax.rem(a + 4 - s, 4)
        arrived(row.at[b, src], rr.at[b, src]).wait()
        loop(1, 4, lambda k: xcopy(k, src).start())

    loop(1, 4, forward)
    arrived(land.at[1 - core], sbr).wait()

    w = land[...].astype(F32)
    w = jnp.stack([w[0], w[1]], axis=1).reshape(D, 384)
    units[...] = jnp.transpose(w).astype(BF).reshape(8, HD, D)

    def each_u1(act):
        for i in range(3):
            part, h = head_unit(lon, i)
            slot = part * 4 + lax.rem(h, 4)
            g = h // 4

            @pl.when(lax.rem(h, 2) == core)
            def _():
                def dest(dyi):
                    t = dyi * 4 + lax.rem(g - b + 4, 4)
                    p, q = shifted(lat, lon, t, 1)
                    far = remote(units.at[i], u1.at[slot], u1s.at[i, dyi], u1r.at[slot], p, q)

                    @pl.when(t == 0)
                    def _():
                        if act == "start":
                            pltpu.make_async_copy(units.at[i], u1.at[slot], u1r.at[slot]).start()

                    @pl.when(t != 0)
                    def _():
                        if act == "start":
                            far.start()
                        else:
                            far.wait_send()

                loop(0, 4, dest)

    each_u1("start")
    loop(1, 16, lambda s: v1copy(s).start())

    sends = lax.rem(b, 2) == core

    def xpeer(s):
        return a * 4 + lax.rem(b + s, 4)

    def wcast(unit, dst, ssem, rsem, act):
        @pl.when(sends)
        def _():
            def along_y(d):
                p, q = shifted(lat, lon, 4 * d, 1)
                c = remote(units.at[unit], dst.at[lon], ssem.at[0, d], rsem.at[lon], p, q)
                act(c)

            def along_x(k):
                c = remote(units.at[unit], dst.at[lon], ssem.at[k, 0], rsem.at[lon], lat, xpeer(k))
                act(c)

            loop(1, 4, along_y)
            loop(1, 4, along_x)

    def wpass(dst, ssem, rsem, act, wait):
        @pl.when(sends)
        def _():
            def one(d):
                slot = lax.rem(a + d, 4) * 4 + b
                if wait:
                    arrived(dst.at[slot], rsem.at[slot]).wait()
                loop(
                    1, 4,
                    lambda k: act(remote(dst.at[slot], dst.at[slot], ssem.at[k, d], rsem.at[slot], lat, xpeer(k))),
                )

            loop(1, 4, one)

    def go(c):
        c.start()

    def left(c):
        c.wait_send()

    def wbegin(unit, dst, ssem, rsem):
        wcast(unit, dst, ssem, rsem, go)

        @pl.when(sends)
        def _():
            pltpu.make_async_copy(units.at[unit], dst.at[lon], rsem.at[lon]).start()

    def wshare(dst, rsem, fsem, k):
        slot = 2 * k + core
        return remote(dst.at[slot], dst.at[slot], fsem.at[k], rsem.at[slot], sib, lon)

    def wforward(dst, rsem, fsem):
        def one(k):
            slot = 2 * k + core

            @pl.when(jnp.logical_not((lax.rem(slot, 4) == b) & (slot // 4 != a)))
            def _():
                arrived(dst.at[slot], rsem.at[slot]).wait()

            wshare(dst, rsem, fsem, k).start()

        loop(0, 8, one)

    def wrest(dst, rsem):
        loop(0, 8, lambda k: arrived(dst.at[2 * k + 1 - core], rsem.at[2 * k + 1 - core]).wait())

    def u2slot(j, i):
        u = j * 3 + i
        part, h = u // 16, lax.rem(u, 16)
        here = h // 8 == core
        here = here if i == 0 else here & (lax.rem(place, 2) == i - 1)
        return here, part * 8 + lax.rem(h, 8)

    def u2do(act):
        for i in range(3):
            here, slot = u2slot(lon, i)

            @pl.when(here)
            def _():
                def along_y(d):
                    p, q = shifted(lat, lon, 4 * d, 1)
                    act(remote(units.at[4 + i], u2.at[slot], u2s.at[i, 0, d], u2r.at[slot], p, q))

                def along_x(k):
                    act(remote(units.at[4 + i], u2.at[slot], u2s.at[i, k, 0], u2r.at[slot], lat, xpeer(k)))

                loop(1, 4, along_y)
                loop(1, 4, along_x)
                if act is go:
                    pltpu.make_async_copy(units.at[4 + i], u2.at[slot], u2r.at[slot]).start()

    def u2on(act):
        def one(d):
            for i in range(3):
                here, slot = u2slot(lax.rem(a + d, 4) * 4 + b, i)

                @pl.when(here)
                def _():
                    if act is go:
                        arrived(u2.at[slot], u2r.at[slot]).wait()
                    loop(
                        1, 4,
                        lambda k: act(remote(u2.at[slot], u2.at[slot], u2s.at[i, k, d], u2r.at[slot], lat, xpeer(k))),
                    )

        loop(1, 4, one)

    zsib = lat + 2 - 4 * lax.rem(place, 2)

    def u2class(k):
        return lax.rem((k // 8) * 16 + core * 8 + lax.rem(k, 8), 3)

    def u2early(k):
        j = ((k // 8) * 16 + core * 8 + lax.rem(k, 8)) // 3
        here = u2class(k) != 2 - lax.rem(place, 2)
        return here & (lax.rem(j, 4) == b) & (j // 4 != a)

    def u2wait(k):
        @pl.when(jnp.logical_not(u2early(k)))
        def _():
            arrived(u2.at[k], u2r.at[k]).wait()

    def u2share(k):
        return remote(u2.at[k], u2.at[k], u2f.at[k], u2r.at[k], zsib, lon)

    def u2pass(act, lo=0, hi=24):
        def one(k):
            @pl.when(u2class(k) == 1 + lax.rem(place, 2))
            def _():
                if act == "start":
                    u2wait(k)
                    u2share(k).start()
                else:
                    u2share(k).wait_send()

        loop(lo, hi, one)

    def u2rest(k):
        @pl.when(u2class(k) != 1 + lax.rem(place, 2))
        def _():
            u2wait(k)

    def u1slot(k, c):
        return (k // 2) * 4 + lax.rem(k, 2) * 2 + c

    def u1share(k):
        slot = u1slot(k, core)
        return remote(u1.at[slot], u1.at[slot], u1f.at[k], u1r.at[slot], sib, lon)

    def u1forward(k):
        slot = u1slot(k, core)
        arrived(u1.at[slot], u1r.at[slot]).wait()
        u1share(k).start()

    u2do(go)
    loop(1, 16, lambda s: v2copy(s).start())
    loop(0, 6, u1forward)
    u2on(go)
    wbegin(3, wo1, w1s, w1r)
    loop(1, 16, lambda s: arrived(vl.at[lax.rem(lon + s, 16)], v1r.at[lax.rem(lon + s, 16)]).wait())

    def collect(s):
        src = lax.rem(b + s, 4)
        loop(0, 4, lambda aa: arrived(row.at[src, aa], rr.at[src, aa]).wait())

    loop(1, 4, collect)
    loop(0, 6, lambda k: arrived(u1.at[u1slot(k, 1 - core)], u1r.at[u1slot(k, 1 - core)]).wait())

    qkv = nt(u1[...].reshape(576, D), row[...].reshape(1024, D)).astype(BF)
    for h in range(4):
        for qb in range(4):
            q_s[qb, h] = qkv[h * HD : (h + 1) * HD, qb * 256 : (qb + 1) * 256]
        kv_s[h] = qkv[192 + h * HD : 192 + (h + 1) * HD]
        kv_s[4 + h] = qkv[384 + h * HD : 384 + (h + 1) * HD]
    ka1 = jnp.concatenate(
        [vl[(2 * (j % 2)) * 4 + j // 2] + vl[(2 * (j % 2) + 1) * 4 + j // 2] for j in range(8)], axis=1
    )
    qa1 = jnp.where(iota((16, 256), 0) == 0, 1.0, 0.0).astype(BF)
    o_s[...] = jnp.zeros_like(o_s)

    def ocopy(bb, aa):
        return remote(o_s.at[bb, aa], land_o.at[lon], os.at[bb, aa], orr.at[lon], lat, aa * 4 + bb)

    def block(step):
        qb = lax.rem(b + 1 + step, 4)

        def head(h):
            k_aug = jnp.concatenate([kv_s[h], ka1], axis=0)
            q_aug = jnp.concatenate([q_s[qb, h], qa1], axis=0)
            v_aug = jnp.concatenate([kv_s[4 + h], jnp.ones((16, 1024), BF)], axis=0)
            t_s[h] = soft(k_aug, q_aug, v_aug)

        loop(0, 4, head)
        o = jnp.transpose(t_s[...].reshape(192, 256)).astype(BF)
        for aa in range(4):
            o_s[qb, aa, :, :192] = o[aa * 64 : (aa + 1) * 64]

        def send(k):
            aa = lax.rem(a + 1 + k, 4)

            @pl.when(aa * 4 + qb != lon)
            def _():
                ocopy(qb, aa).start()

        loop(0, 4, send)
        u2pass("start", step * 6, step * 6 + 6)

        @pl.when(step == 1)
        def _():
            wpass(wo1, w1s, w1r, go, True)


    loop(0, 4, block)

    def mwait(s):
        src = lax.rem(place + 16 - s, 16)
        arrived(mv.at[core, src], v2r.at[core, src]).wait()

    loop(1, 16, mwait)
    mshare = remote(mv.at[core], mv.at[core], v2s.at[0], v2r.at[core, 0], sib, lon)
    mshare.start()
    land_o[lon] = o_s[b, a]
    wforward(wo1, w1r, w1f)
    loop(1, 16, lambda s: arrived(land_o.at[lax.rem(lon + s, 16)], orr.at[lax.rem(lon + s, 16)]).wait())
    wrest(wo1, w1r)

    heads = jnp.concatenate(
        [
            jnp.concatenate([land_o[4 * k + g][:, :192] for g in range(4)], axis=1)
            for k in range(4)
        ],
        axis=0,
    )
    middle = start_s[...] + nt(heads, wo1[...].reshape(D, D))
    start_s[...] = middle

    i = lax.broadcasted_iota(jnp.int32, (256, 256), 0)
    j = lax.broadcasted_iota(jnp.int32, (256, 256), 1)
    from_row = ((i >> 2) & 3) * 64 + (i >> 4) * 4 + (i & 3)
    perm = jnp.where(from_row == j, 1.0, 0.0).astype(BF)
    xn2 = jnp.dot(perm, normalize(middle, g2[...].reshape(1, D)), preferred_element_type=F32).astype(BF)
    x2_s[...] = xn2.reshape(16, 16, D)

    def x2copy(s):
        to = lax.rem(place + s, 16)
        return remote(
            x2_s.at[to], col.at[core, place], x2s.at[s], x2r.at[core, place], to * 2 + core, lon
        )

    def x2share(src):
        return remote(col.at[core, src], col.at[core, src], x2f.at[src], x2r.at[core, src], sib, lon)

    loop(1, 16, lambda s: x2copy(s).start())
    col[core, place] = x2_s[place]
    x2share(place).start()

    def x2forward(s):
        src = lax.rem(place + 16 - s, 16)
        arrived(col.at[core, src], x2r.at[core, src]).wait()
        x2share(src).start()

    loop(1, 16, x2forward)
    wbegin(7, wo2, w2s, w2r)

    arrived(mv.at[1 - core], v2r.at[1 - core, 0]).wait()
    loop(0, 24, u2rest)
    loop(0, 16, lambda k: arrived(col.at[1 - core, k], x2r.at[1 - core, k]).wait())

    qkv2[...] = nt(u2[...].reshape(1152, D), col[...].reshape(512, D)).astype(BF).reshape(24, HD, 512)
    first = jnp.where((iota((16, 128), 0) == 0) & (iota((16, 128), 1) < 4), 1.0, 0.0).astype(BF)
    fr = iota((16, 512), 0)
    same = (iota((16, 512), 1) & 3) == fr - 1
    ka2 = (nt(first, mv[...].reshape(512, 128)) + jnp.where(same, 1.0, 0.0)).astype(BF)
    other = (fr >= 1) & (fr <= 4) & jnp.logical_not(same)
    qa2 = jnp.where(fr == 0, 1.0, jnp.where(other, -1e34, 0.0)).astype(BF)

    def head2(h):
        k_aug = jnp.concatenate([qkv2[8 + h], ka2], axis=0)
        q_aug = jnp.concatenate([qkv2[h], qa2], axis=0)
        v_aug = jnp.concatenate([qkv2[16 + h], jnp.ones((16, 512), BF)], axis=0)
        t2[h] = soft(k_aug, q_aug, v_aug)

    loop(0, 8, head2)
    wpass(wo2, w2s, w2r, go, True)
    o2_s[...] = jnp.transpose(t2[...].reshape(384, 512)).astype(BF).reshape(2, 16, 16, 384)

    def bcopy(s):
        to = lax.rem(lat + s, NLAT)
        return remote(
            o2_s.at[lax.rem(to, 2), to // 2], back.at[core, place], bs.at[s], br.at[core, place], to, lon
        )

    loop(1, NLAT, lambda s: bcopy(s).start())
    back[core, place] = o2_s[core, place]
    wforward(wo2, w2r, w2f)

    def bwait(s):
        src = lax.rem(lat + NLAT - s, NLAT)
        c, p = lax.rem(src, 2), src // 2
        arrived(back.at[c, p], br.at[c, p]).wait()

    loop(1, NLAT, bwait)
    wrest(wo2, w2r)
    heads2 = jnp.concatenate([back[0].reshape(256, 384), back[1].reshape(256, 384)], axis=1)
    heads2 = lax.dot_general(
        perm, heads2, (((0,), (0,)), ((), ())), preferred_element_type=F32
    ).astype(BF)
    out[...] = (start_s[...] + nt(heads2, wo2[...].reshape(D, D))).astype(BF).reshape(4, 64, D)

    loop(1, 16, lambda s: wcopy(s).wait_send())
    sibling.wait_send()
    loop(1, 16, lambda s: v1copy(s).wait_send())
    loop(1, 16, lambda s: v2copy(s).wait_send())
    mshare.wait_send()
    loop(1, 4, lambda s: ycopy(s).wait_send())
    loop(1, 4, lambda s: loop(0, 4, lambda aa: xcopy(s, aa).wait_send()))
    each_u1("finish")
    loop(0, 6, lambda k: u1share(k).wait_send())

    wcast(3, wo1, w1s, w1r, left)
    wpass(wo1, w1s, w1r, left, False)
    wcast(7, wo2, w2s, w2r, left)
    wpass(wo2, w2s, w2r, left, False)

    loop(0, 8, lambda k: wshare(wo1, w1r, w1f, k).wait_send())
    loop(0, 8, lambda k: wshare(wo2, w2r, w2f, k).wait_send())
    u2do(left)
    u2on(left)
    u2pass("finish")

    def osent(k):
        bb, aa = lax.rem(k, 4), k // 4

        @pl.when(k != lon)
        def _():
            ocopy(bb, aa).wait_send()

    loop(0, 16, osent)
    loop(1, 16, lambda s: x2copy(s).wait_send())
    loop(0, 16, lambda k: x2share(k).wait_send())
    loop(1, NLAT, lambda s: bcopy(s).wait_send())


def pair(*args):
    return pl.pallas_call(
        pair_kernel,
        out_shape=jax.ShapeDtypeStruct((4, 64, D), BF),
        in_specs=[VMEM] * len(args),
        out_specs=VMEM,
        scratch_shapes=[
            pltpu.VMEM((24, 384), BF),
            pltpu.VMEM((8, D), F32),
            pltpu.VMEM((4, 16, 128), BF),
            pltpu.VMEM((16, 16, 128), BF),
            pltpu.VMEM((2, 16, 24, 384), BF),
            pltpu.VMEM((8, HD, D), BF),
            pltpu.VMEM((256, D), F32),
            pltpu.VMEM((4, 64, D), BF),
            pltpu.VMEM((4, 4, 64, D), BF),
            pltpu.VMEM((12, HD, D), BF),
            pltpu.VMEM((16, HD, D), BF),
            pltpu.VMEM((24, HD, D), BF),
            pltpu.VMEM((16, HD, D), BF),
            pltpu.VMEM((16, 16, 128), BF),
            pltpu.VMEM((2, 16, 16, 128), BF),
            pltpu.VMEM((4, 4, HD, 256), BF),
            pltpu.VMEM((8, HD, 1024), BF),
            pltpu.VMEM((4, HD, 256), F32),
            pltpu.VMEM((4, 4, 64, 256), BF),
            pltpu.VMEM((16, 64, 256), BF),
            pltpu.VMEM((16, 16, D), BF),
            pltpu.VMEM((2, 16, 16, D), BF),
            pltpu.VMEM((24, HD, 512), BF),
            pltpu.VMEM((8, HD, 512), F32),
            pltpu.VMEM((2, 16, 16, 384), BF),
            pltpu.VMEM((2, 16, 16, 384), BF),
            DMA((16,)), DMA((16,)), DMA, DMA, DMA((16,)), DMA((16,)), DMA((NLAT,)), DMA((2, 16)),
            DMA((4,)), DMA((4, 4)), DMA((4, 4)), DMA((3, 4)), DMA((12,)), DMA((6,)),
            DMA((4, 4)), DMA((16,)), DMA((8,)), DMA((3, 4, 4)), DMA((24,)), DMA((24,)),
            DMA((4, 4)), DMA((16,)), DMA((8,)), DMA((4, 4)), DMA((16,)),
            DMA((16,)), DMA((2, 16)), DMA((16,)), DMA((NLAT,)), DMA((2, 16)),
        ],
        compiler_params=pltpu.CompilerParams(
            collective_id=0, has_side_effects=True, vmem_limit_bytes=LIMIT
        ),
    )(*args)


def local(
    tokens, source_id, valid, source_table, gain_lon, gain_lat, wqkv_lon, wout_lon, wqkv_lat, wout_lat
):
    return pair(
        tokens, source_id, valid, source_table, gain_lon, gain_lat, wqkv_lon, wout_lon, wqkv_lat, wout_lat
    )


def solution(mesh):
    placed = (
        P("lat", "lon", None),
        P("lat", "lon"),
        P("lat", "lon"),
        P(),
        P(),
        P(),
        P("lat", "lon"),
        P("lat", "lon"),
        P("lat", "lon"),
        P("lat", "lon"),
    )
    return jax.shard_map(
        local, mesh=mesh, in_specs=placed, out_specs=P("lat", "lon", None), check_vma=False
    )
```
